256 devices in a mesh: group: 8 (over x, core), inner: 32 (over z, y).
Axes of the slice: x: 4, y: 4, z: 8, core: 2. Of those that a mesh axis runs over, the one named last changes fastest.
Arguments:
- features: bfloat16 [524288, 256], P(('group', 'inner')), may hold values from -6 to 6
- w_self: bfloat16 [256, 256], replicated, may hold values from -0.375 to 0.375
- w_neigh: bfloat16 [256, 256], replicated, may hold values from -0.375 to 0.375
- node_bias: float32 [256], replicated, may hold values from -3 to 3
- grad_out: bfloat16 [524288, 256], P(('group', 'inner')), may hold values from -6 to 6
- send_rows: int32 [256, 32, 8, 8], P(('group', 'inner')), may hold values from 0 to 2047
- send_count: int32 [256, 32, 8], P(('group', 'inner')), may hold values from 0 to 8, as said below
- adjacency: int32 [256, 16, 2, 128, 128], P(('group', 'inner')), may hold values from 0 to 2
- tile_source: int32 [256, 16, 2], P(('group', 'inner')), may hold values from 0 to 31, as said below
Outputs:
- output: bfloat16 [524288, 256], P(('group', 'inner'))
- grad_features: bfloat16 [524288, 256], P(('group', 'inner'))
- grad_self: float32 [256, 256], replicated
- grad_neigh: float32 [256, 256], replicated
- grad_bias: float32 [256], replicated
The draws below stay inside these ranges and needn't reach their ends.
Inputs may be any that keep to these rules, and one draw needn't show every extreme that they name: `send_count`: A device's block to itself is empty; each device fills all 8 slots of its block to the next device of its own group; the other blocks within a group hold at least half of the slots. `tile_source`: the first tile of each destination block reads a block of the device's own rows, the others read blocks of halo rows.
All inputs are finite; a program needn't handle non-finite values.
Results may differ from the reference program's by a relative error of at most 0.0075.
Values may be sent and summed in bfloat16 or wider, within the bound.
A program may use at most 64 MiB of HBM per device.

```python
import math
import jax
import jax.numpy as jnp
from jax import lax

H = 256
NL = 2048
BX = 8
K = 2
TILE = 128
NODES = 524288
DST_BLOCKS = 16
HALO = 2048
EXTENDED = 4096
EXT_BLOCKS = 32
N_GROUP = 8
N_INNER = 32
DEVICES = 256


def draw_send_count(key, part):
    key = jax.random.fold_in(key, 11)
    first_key, second_key = jax.random.split(key)
    shape = (DEVICES, N_INNER, N_GROUP)
    device_id = lax.broadcasted_iota(jnp.int32, shape, 0)
    own_group = device_id // N_INNER
    own_inner = device_id % N_INNER
    peer_inner = lax.broadcasted_iota(jnp.int32, shape, 1)
    peer_group = lax.broadcasted_iota(jnp.int32, shape, 2)
    same_group = peer_group == own_group
    nearby = jax.random.randint(first_key, shape, BX // 2, BX + 1)
    distant = jax.random.randint(second_key, shape, 0, BX + 1)
    counts = jnp.where(same_group, nearby, distant)
    counts = jnp.where(same_group & (peer_inner == own_inner), 0, counts)
    counts = jnp.where(same_group & (peer_inner == (own_inner + 1) % N_INNER), BX, counts)
    return counts.astype(jnp.int32)


def draw_adjacency(key, part):
    key = jax.random.fold_in(key, 23)
    alive_key, edge_key, weight_key = jax.random.split(key, 3)
    shape = (DEVICES, DST_BLOCKS, K, TILE, TILE)
    alive = jax.random.randint(alive_key, (DEVICES, DST_BLOCKS, 1, TILE, 1), 0, 16) > 0
    edges = jax.random.randint(edge_key, shape, 0, 16) == 0
    multiple = jax.random.randint(weight_key, shape, 1, 3)
    return jnp.where(alive & edges, multiple, 0).astype(jnp.int32)


def draw_tile_source(key, part):
    key = jax.random.fold_in(key, 37)
    local_key, remote_key = jax.random.split(key)
    shape = (DEVICES, DST_BLOCKS, K)
    position = lax.broadcasted_iota(jnp.int32, shape, 2)
    own_block = jax.random.randint(local_key, shape, 0, DST_BLOCKS)
    halo_block = jax.random.randint(remote_key, shape, DST_BLOCKS, EXT_BLOCKS)
    return jnp.where(position == 0, own_block, halo_block).astype(jnp.int32)


def plant(values, stream_key, smallest, high):
    dims = values.shape
    index_at = [jax.random.randint(jax.random.fold_in(stream_key, axis), (), 0, dims[axis]) for axis in range(len(dims))]
    values = values.at[tuple(index_at)].set(smallest)
    longest = dims.index(max(dims))
    index_at[longest] = (index_at[longest] + 1) % dims[longest]
    return values.at[tuple(index_at)].set(high)


def level_of(key, dims, pieces, low, largest):
    loudness, own = 1.0, jax.random.fold_in(key, 6)
    for axis_at, blocks in pieces:
        heights = jnp.exp(jax.random.uniform(jax.random.fold_in(own, axis_at), (blocks,), jnp.float32, low / len(pieces), largest / len(pieces)))
        loudness = loudness * jnp.repeat(heights, dims[axis_at] // blocks).reshape([-1 if axis == axis_at else 1 for axis in range(len(dims))])
    return loudness


def centred(key, shape, spread, most, cuts=(), held_as=jnp.bfloat16):
    factor_of = level_of(key, shape, cuts, -0.22, 0.18) if cuts else 1.0
    entries = jax.random.normal(key, shape, jnp.float32) * spread * factor_of
    return jnp.minimum(jnp.maximum(entries, -most), most).astype(held_as)


def setup_inputs(seed: int = 0) -> dict:
    arg_keys = jax.random.split(jax.random.key(seed), 10)
    return {
        "features": centred(arg_keys[0], (NODES, H), 1.0, 6.0, ((0, 256),)),
        "w_self": centred(arg_keys[1], (H, H), H ** -0.5, 0.375),
        "w_neigh": centred(arg_keys[2], (H, H), H ** -0.5, 0.375),
        "node_bias": centred(arg_keys[3], (H,), 0.5, 3.0, (), jnp.float32),
        "grad_out": centred(arg_keys[4], (NODES, H), 1.0, 6.0, ((0, 256),)),
        "send_rows": plant(jax.random.randint(arg_keys[5], (DEVICES, N_INNER, N_GROUP, BX), 0, NL), jax.random.fold_in(arg_keys[5], 1), 0, NL - 1).astype(jnp.int32),
        "send_count": draw_send_count(jax.random.fold_in(arg_keys[9], 71), 0),
        "adjacency": draw_adjacency(jax.random.fold_in(arg_keys[9], 71), 0),
        "tile_source": draw_tile_source(jax.random.fold_in(arg_keys[9], 71), 0),
    }


def reference(features, w_self, w_neigh, node_bias, grad_out, send_rows, send_count, adjacency, tile_source):
    devices = N_GROUP * N_INNER
    feat_all = features.reshape(devices, NL, H)
    grad_all = grad_out.reshape(devices, NL, H)
    slot_iota = lax.broadcasted_iota(jnp.int32, send_rows.shape, 3)
    valid = slot_iota < send_count[..., None]

    def pick(operands):
        table, index, keep = operands
        gathered = table[index.reshape(-1)].reshape(N_INNER, N_GROUP, BX, H)
        return jnp.where(keep[..., None], gathered, jnp.zeros((), gathered.dtype))
    outgoing = lax.map(pick, (feat_all, send_rows, valid))
    sixfold = outgoing.reshape(N_GROUP, N_INNER, N_INNER, N_GROUP, BX, H)
    halo_all = jnp.transpose(sixfold, (3, 2, 1, 0, 4, 5)).reshape(devices, HALO, H)

    def local(operands):
        feat_dev, halo_dev, grad_dev, adj_dev, source_dev = operands
        extended = jnp.concatenate([feat_dev, halo_dev], axis=0)
        blocks = extended.reshape(EXT_BLOCKS, TILE, H)
        picked = blocks[source_dev]
        adj_float = adj_dev.astype(jnp.float32)
        summed = jnp.einsum('dkrc,dkch->drh', adj_float, picked.astype(jnp.float32))
        degree = lax.optimization_barrier(jnp.sum(adj_dev, axis=(1, 3)))
        inverse = 1.0 / jnp.maximum(degree, 1).astype(jnp.float32)
        mean_agg = (summed * inverse[..., None]).reshape(NL, H).astype(jnp.bfloat16)
        pre = jnp.dot(feat_dev, w_self, preferred_element_type=jnp.float32)
        pre = pre + jnp.dot(mean_agg, w_neigh, preferred_element_type=jnp.float32) + node_bias
        sigma = jax.nn.sigmoid(pre)
        result = (pre * sigma).astype(jnp.bfloat16)
        slope = sigma * (1.0 + pre * (1.0 - sigma))
        grad_pre = (grad_dev.astype(jnp.float32) * slope).astype(jnp.bfloat16)
        part_self = jnp.dot(feat_dev.T, grad_pre, preferred_element_type=jnp.float32)
        part_neigh = jnp.dot(mean_agg.T, grad_pre, preferred_element_type=jnp.float32)
        part_bias = lax.optimization_barrier(jnp.sum(grad_pre.astype(jnp.float32), axis=0))
        back_self = jnp.dot(grad_pre, w_self.T, preferred_element_type=jnp.float32)
        back_agg = jnp.dot(grad_pre, w_neigh.T, preferred_element_type=jnp.float32)
        back_agg = (back_agg.reshape(DST_BLOCKS, TILE, H) * inverse[..., None]).astype(jnp.bfloat16)
        picked_grad = jnp.einsum('dkrc,drh->dkch', adj_float, back_agg.astype(jnp.float32))
        ext_grad = jnp.zeros((EXT_BLOCKS, TILE, H), jnp.float32)
        ext_grad = ext_grad.at[source_dev.reshape(-1)].add(picked_grad.reshape(-1, TILE, H)).reshape(EXTENDED, H)
        halo_grad = ext_grad[NL:].astype(jnp.bfloat16)
        base = back_self + ext_grad[:NL]
        return (result, part_self, part_neigh, part_bias, base, halo_grad)
    results = lax.map(local, (feat_all, halo_all, grad_all, adjacency, tile_source))
    output, part_self, part_neigh, part_bias, base, halo_grad = results
    factor = 1.0 / math.sqrt(NODES)
    grad_self = lax.optimization_barrier(jnp.sum(part_self, axis=0)) * factor
    grad_neigh = lax.optimization_barrier(jnp.sum(part_neigh, axis=0)) * factor
    grad_bias = lax.optimization_barrier(jnp.sum(part_bias, axis=0)) * factor
    sixback = halo_grad.reshape(N_GROUP, N_INNER, N_INNER, N_GROUP, BX, H)
    returned_all = jnp.transpose(sixback, (3, 2, 1, 0, 4, 5)).reshape(devices, N_INNER, N_GROUP, BX, H)

    def settle(operands):
        base_dev, back_dev, index, keep = operands
        masked = jnp.where(keep[..., None], back_dev.astype(jnp.float32), jnp.zeros((), jnp.float32))
        total = base_dev.at[index.reshape(-1)].add(masked.reshape(-1, H))
        return total.astype(jnp.bfloat16)
    grad_features = lax.map(settle, (base, returned_all, send_rows, valid))
    return (output.reshape(NODES, H), grad_features.reshape(NODES, H), grad_self, grad_neigh, grad_bias)
```

```python
import math

import jax
import jax.numpy as jnp
from jax import lax
from jax.experimental import pallas as pl
from jax.experimental.pallas import tpu as pltpu
from jax.sharding import PartitionSpec as P

MESH = pl.DeviceIdType.MESH


def contract_rows(left, right):
    return lax.dot_general(
        left, right, (((0,), (0,)), ((), ())), preferred_element_type=jnp.float32
    )


def contract_cols(left, right):
    return lax.dot_general(
        left, right, (((1,), (1,)), ((), ())), preferred_element_type=jnp.float32
    )


def exchange_kernel(x, y, ssem, rsem, lsem):
    g, j = lax.axis_index("group"), lax.axis_index("inner")
    z, yy, cx, cc = j // 4, j % 4, g // 2, g % 2
    me = j * 8 + g
    own = pltpu.make_async_copy(x.at[me], y.at[me], lsem)
    own.start()
    barrier = pltpu.get_barrier_semaphore()

    def greet(t, carry):
        d = lax.rem(me + t, 256)
        pl.semaphore_signal(barrier, inc=1, device_id=(d % 8, d // 8), device_id_type=MESH)
        return carry

    lax.fori_loop(1, 256, greet, 0)
    pl.semaphore_wait(barrier, 255)
    for k in range(8):
        dz = (4, 3, 5, 2, 6, 1, 7, 0)[k]

        def send(m, carry):
            h = ((cx + m // 8) % 4) * 2 + (cc + m // 4) % 2
            i = ((z + dz) % 8) * 4 + (yy + m) % 4
            pltpu.make_async_remote_copy(
                x.at[i * 8 + h], y.at[me], ssem.at[k], rsem.at[k], device_id=(h, i), device_id_type=MESH
            ).start()
            return carry

        lax.fori_loop(1 if dz == 0 else 0, 32, send, 0)
    for k in range(8):
        n = 31 if k == 7 else 32
        part = pltpu.make_async_remote_copy(
            x.at[pl.ds(0, n)], y.at[pl.ds(0, n)], ssem.at[k], rsem.at[k], device_id=(g, j), device_id_type=MESH
        )
        part.wait()
    own.wait()


def exchange(x, cid):
    inner, group, slots, width = x.shape
    t = x.reshape(inner * group, slots, 2, width // 2).transpose(0, 2, 1, 3).reshape(inner * group, 2 * slots, width // 2)
    y = pl.pallas_call(
        exchange_kernel,
        out_shape=jax.ShapeDtypeStruct(t.shape, t.dtype),
        in_specs=[pl.BlockSpec(memory_space=pltpu.VMEM)],
        out_specs=pl.BlockSpec(memory_space=pltpu.VMEM),
        scratch_shapes=[pltpu.SemaphoreType.DMA((8,)), pltpu.SemaphoreType.DMA((8,)), pltpu.SemaphoreType.DMA],
        compiler_params=pltpu.CompilerParams(collective_id=0, has_side_effects=True, vmem_limit_bytes=16 << 20),
    )(t)
    return y.reshape(inner, group, 2, slots, width // 2).transpose(0, 1, 3, 2, 4).reshape(x.shape)

def local(
    features, w_self, w_neigh, node_bias, grad_out, send_rows, send_count, adjacency, tile_source
):
    node_count, width = features.shape
    slot_rows = send_rows[0]
    inner_count, group_count, slots = slot_rows.shape
    keep_slot = lax.broadcasted_iota(jnp.int32, slot_rows.shape, 2) < send_count[0][:, :, None]
    gathered = features[slot_rows.reshape(-1)].reshape(inner_count, group_count, slots, width)
    outgoing = jnp.where(keep_slot[..., None], gathered, jnp.zeros((), jnp.bfloat16))
    halo_rows = exchange(outgoing, 0)
    extended = jnp.concatenate([features, halo_rows.reshape(-1, width)], axis=0)
    tile_edge = adjacency.shape[-1]
    blocks = extended.reshape(-1, tile_edge, width)
    sources = tile_source[0]
    picked = blocks[sources]
    adj_tiles = adjacency[0]
    adj_values = adj_tiles.astype(jnp.bfloat16)
    summed = jnp.einsum("dkrc,dkch->drh", adj_values, picked, preferred_element_type=jnp.float32)
    degree = jnp.sum(adj_tiles, axis=(1, 3))
    inverse = 1.0 / jnp.maximum(degree, 1).astype(jnp.float32)
    mean_agg = (summed * inverse[..., None]).reshape(node_count, width).astype(jnp.bfloat16)
    pre_act = jnp.dot(features, w_self, preferred_element_type=jnp.float32)
    pre_act = pre_act + jnp.dot(mean_agg, w_neigh, preferred_element_type=jnp.float32) + node_bias
    sigma = jax.nn.sigmoid(pre_act)
    output = (pre_act * sigma).astype(jnp.bfloat16)
    slope = sigma * (1.0 + pre_act * (1.0 - sigma))
    grad_pre = (grad_out.astype(jnp.float32) * slope).astype(jnp.bfloat16)
    part_self = contract_rows(features, grad_pre)
    part_neigh = contract_rows(mean_agg, grad_pre)
    part_bias = jnp.sum(grad_pre.astype(jnp.float32), axis=0)
    summed_grads = lax.psum((part_self, part_neigh, part_bias), ("group", "inner"))
    factor = 1.0 / math.sqrt(node_count * lax.axis_size("group") * lax.axis_size("inner"))
    back_self = contract_cols(grad_pre, w_self)
    back_agg = contract_cols(grad_pre, w_neigh).reshape(-1, tile_edge, width)
    back_agg = (back_agg * inverse[..., None]).astype(jnp.bfloat16)
    picked_grad = jnp.einsum(
        "dkrc,drh->dkch", adj_values, back_agg, preferred_element_type=jnp.float32
    )
    ext_grad = jnp.zeros(blocks.shape, jnp.float32)
    ext_grad = ext_grad.at[sources.reshape(-1)].add(picked_grad.reshape(-1, tile_edge, width))
    ext_grad = ext_grad.reshape(-1, width)
    halo_grad = (
        ext_grad[node_count:].reshape(inner_count, group_count, slots, width).astype(jnp.bfloat16)
    )
    returned = exchange(halo_grad, 1)
    masked = jnp.where(
        keep_slot[..., None], returned.astype(jnp.float32), jnp.zeros((), jnp.float32)
    )
    grad_total = back_self + ext_grad[:node_count]
    grad_total = grad_total.at[slot_rows.reshape(-1)].add(masked.reshape(-1, width))
    return (
        output,
        grad_total.astype(jnp.bfloat16),
        summed_grads[0] * factor,
        summed_grads[1] * factor,
        summed_grads[2] * factor,
    )


def solution(mesh):
    placed = (
        P(("group", "inner"), None),
        P(),
        P(),
        P(),
        P(("group", "inner"), None),
        P(("group", "inner"), None, None, None),
        P(("group", "inner"), None, None),
        P(("group", "inner"), None, None, None, None),
        P(("group", "inner"), None, None),
    )
    return jax.shard_map(
        local,
        mesh=mesh,
        in_specs=placed,
        out_specs=(P(("group", "inner"), None), P(("group", "inner"), None), P(), P(), P()),
        check_vma=False,
    )
```

```python
import math

import jax
import jax.numpy as jnp
from jax import lax
from jax.experimental import pallas as pl
from jax.experimental.pallas import tpu as pltpu
from jax.sharding import PartitionSpec as P

MESH = pl.DeviceIdType.MESH
BF16, F32 = jnp.bfloat16, jnp.float32
ROWS, WIDTH, EDGE, TILES = 2048, 256, 128, 16
PARTS = 17
STEPS = (4, 3, 5, 2, 6, 1, 7, 0)


def dot(left, right):
    return jnp.dot(left, right, preferred_element_type=F32)


def dot_rows(left, right):
    return lax.dot_general(left, right, (((0,), (0,)), ((), ())), preferred_element_type=F32)


def dot_cols(left, right):
    return lax.dot_general(left, right, (((1,), (1,)), ((), ())), preferred_element_type=F32)


def to_blocks(rows):
    left = rows[:, :128].reshape(32, 8, 128)
    right = rows[:, 128:].reshape(32, 8, 128)
    return jnp.concatenate([left, right], axis=1).astype(BF16)


def from_blocks(blocks):
    wide = blocks.astype(F32)
    rows = jnp.concatenate([wide[:, :8], wide[:, 8:]], axis=2)
    return rows.reshape(256, 256).astype(BF16)


def kernel(
    idx_ref, ts_ref, bias_ref, ws_ref, wn_ref, feat_hbm, gout_hbm, adj_hbm,
    out_hbm, gf_hbm, gs_ref, gn_ref, gb_ref,
    feat, gout, adj, col, outb, halob, outg, retb, halo, adj1, at_own, at_halo, inv,
    s_own, p_self, mean, gpre, gagg, total, outv, gfv,
    part, r1buf, r1sum, r2buf, tiles, fin,
    lsem, s1, q1, s2, q2, sr, qr,
):
    g, j = lax.axis_index("group"), lax.axis_index("inner")
    z, y, cx, cc = j // 4, j % 4, g // 2, g % 2
    me = j * 8 + g

    load_feat = pltpu.make_async_copy(feat_hbm, feat, lsem.at[0])
    load_adj = pltpu.make_async_copy(adj_hbm, adj, lsem.at[1])
    load_gout = pltpu.make_async_copy(gout_hbm, gout, lsem.at[2])
    load_feat.start()
    load_adj.start()
    load_gout.start()

    barrier = pltpu.get_barrier_semaphore()

    def greet(t, carry):
        d = lax.rem(me + t, 256)
        pl.semaphore_signal(barrier, inc=1, device_id=(d % 8, d // 8), device_id_type=MESH)
        return carry

    lax.fori_loop(1, 256, greet, 0)

    turned = jnp.transpose(idx_ref[...].astype(F32)).astype(jnp.int32)
    for n in range(16):
        col[n] = jnp.broadcast_to(turned[:, n : n + 1], (128, 128))
    load_feat.wait()

    def pick(n, carry):
        slab = jnp.concatenate([col[2 * n], col[2 * n + 1]], axis=0)
        slab = jnp.concatenate([slab, slab], axis=1)
        lane = lax.broadcasted_iota(jnp.int32, (256, 256), 1)
        acc = jnp.zeros((256, 256), F32)
        for c in range(8):
            hot = jnp.where(slab == lane + 256 * c, 1.0, 0.0).astype(BF16)
            acc = acc + dot(hot, feat[2 * c : 2 * c + 2].reshape(256, 256))
        outb[pl.ds(n * 32, 32)] = to_blocks(acc)
        return carry

    lax.fori_loop(0, 8, pick, 0)
    own1 = pltpu.make_async_copy(outb.at[me], halob.at[me], lsem.at[3])
    own1.start()
    pl.semaphore_wait(barrier, 255)

    def send_plane(k, src, dst, ssem, rsem):
        dz = STEPS[k]

        def send(m, carry):
            h = ((cx + m // 8) % 4) * 2 + (cc + m // 4) % 2
            i = ((z + dz) % 8) * 4 + (y + m) % 4
            pltpu.make_async_remote_copy(
                src.at[i * 8 + h], dst.at[me], ssem.at[k], rsem.at[k], device_id=(h, i), device_id_type=MESH
            ).start()
            return carry

        lax.fori_loop(1 if dz == 0 else 0, 32, send, 0)

    def plane(k, src, dst, ssem, rsem):
        n = 31 if STEPS[k] == 0 else 32
        return pltpu.make_async_remote_copy(
            src.at[pl.ds(0, n)], dst.at[pl.ds(0, n)], ssem.at[k], rsem.at[k], device_id=(g, j), device_id_type=MESH
        )

    for k in range(8):
        send_plane(k, outb, halob, s1, q1)

    load_adj.wait()

    def prepare(b, carry):
        rows = pl.ds(pl.multiple_of(b * EDGE, EDGE), EDGE)
        a0 = adj[b, 0].astype(F32)
        a1 = adj[b, 1].astype(F32)
        degree = jnp.sum(a0 + a1, axis=1, keepdims=True)
        inv[rows, :] = jnp.broadcast_to(1.0 / jnp.maximum(degree, 1.0), (EDGE, EDGE))
        adj1[b] = a1.astype(BF16)
        t0 = ts_ref[b, 0]
        t1 = jnp.maximum(ts_ref[b, 1] - TILES, 0)
        block = feat[t0]
        s_own[rows, :] = dot(a0.astype(BF16), block)
        p_self[rows, :] = dot(feat[b], ws_ref[...]) + bias_ref[...]
        a0t = jnp.transpose(a0)
        a1t = jnp.transpose(a1)
        own = jnp.broadcast_to(t0, (EDGE, EDGE))
        far = jnp.broadcast_to(t1, (EDGE, EDGE))
        for e in range(TILES):
            at_own[e * EDGE : (e + 1) * EDGE, rows] = jnp.where(own == e, a0t, 0.0).astype(BF16)
            at_halo[e * EDGE : (e + 1) * EDGE, rows] = jnp.where(far == e, a1t, 0.0).astype(BF16)
        return carry

    lax.fori_loop(0, TILES, prepare, 0)
    load_gout.wait()

    own1.wait()
    for k in range(8):
        plane(k, outb, halob, s1, q1).wait_recv()
        n = (z + 8 - STEPS[k]) % 8
        halo[pl.ds(2 * n, 2)] = from_blocks(halob[pl.ds(n * 32, 32)]).reshape(2, EDGE, WIDTH)

    def layer(b, carry):
        rows = pl.ds(pl.multiple_of(b * 256, 256), 256)
        sums = []
        for u in range(2):
            t1 = jnp.maximum(ts_ref[2 * b + u, 1] - TILES, 0)
            block = halo[t1]
            sums.append(dot(adj1[2 * b + u], block))
        scale = inv[rows, :]
        scale = jnp.concatenate([scale, scale], axis=1)
        m = ((s_own[rows, :] + jnp.concatenate(sums, axis=0)) * scale).astype(BF16)
        mean[rows, :] = m
        pre = p_self[rows, :] + dot(m, wn_ref[...])
        sigma = 1.0 / (1.0 + jnp.exp(-pre))
        outv[rows, :] = (pre * sigma).astype(BF16)
        slope = sigma * (1.0 + pre * (1.0 - sigma))
        gp = (gout[rows, :].astype(F32) * slope).astype(BF16)
        gpre[rows, :] = gp
        gagg[rows, :] = (dot_cols(gp, wn_ref[...]) * scale).astype(BF16)
        return carry

    lax.fori_loop(0, 8, layer, 0)
    store_out = pltpu.make_async_copy(outv, out_hbm, lsem.at[4])
    store_out.start()

    for k in range(8):
        n = (z + STEPS[k]) % 8
        rows = pl.ds(pl.multiple_of(n * 256, 256), 256)
        acc = jnp.zeros((256, 256), F32)
        for c in range(8):
            acc = acc + dot(at_halo[rows, 256 * c : 256 * c + 256], gagg[256 * c : 256 * c + 256, :])
        outg[pl.ds(n * 32, 32)] = to_blocks(acc)
        send_plane(k, outg, retb, s2, q2)
    own2 = pltpu.make_async_copy(outg.at[me], retb.at[me], lsem.at[5])
    own2.start()

    def weights(c, carry):
        acc_self, acc_neigh, acc_bias = carry
        rows = pl.ds(pl.multiple_of(c * 256, 256), 256)
        gp = gpre[rows, :]
        acc_self = acc_self + dot_rows(feat[pl.ds(2 * c, 2)].reshape(256, 256), gp)
        acc_neigh = acc_neigh + dot_rows(mean[rows, :], gp)
        acc_bias = acc_bias + jnp.sum(gp.astype(F32).reshape(32, 8, 256), axis=0)
        return acc_self, acc_neigh, acc_bias

    zero = jnp.zeros((256, 256), F32)
    acc_self, acc_neigh, acc_bias = lax.fori_loop(0, 8, weights, (zero, zero, jnp.zeros((8, 256), F32)))
    bias_row = jnp.sum(acc_bias, axis=0, keepdims=True)
    bias_tile = jnp.concatenate([bias_row[:, :128], bias_row[:, 128:], jnp.zeros((6, 128), F32)], axis=0)
    for h in range(8):
        acc = acc_self if h < 4 else acc_neigh
        for a in range(8):
            r = (h % 4) * 64 + a * 8
            part[h, 2 * a] = acc[r : r + 8, :128]
            part[h, 2 * a + 1] = acc[r : r + 8, 128:]
        part[h, 16] = bias_tile

    def send_share(t, carry):
        h = (g + t) % 8
        pltpu.make_async_remote_copy(
            part.at[h], r1buf.at[g], sr.at[0], qr.at[0], device_id=(h, j), device_id_type=MESH
        ).start()
        return carry

    lax.fori_loop(1, 8, send_share, 0)
    r1buf[g] = part[g]

    def base(n, carry):
        rows = pl.ds(pl.multiple_of(n * 256, 256), 256)
        acc = dot_cols(gpre[rows, :], ws_ref[...])
        for c in range(8):
            acc = acc + dot(at_own[rows, 256 * c : 256 * c + 256], gagg[256 * c : 256 * c + 256, :])
        total[rows, :] = acc
        return carry

    lax.fori_loop(0, 8, base, 0)

    def settle(k):
        plane(k, outg, retb, s2, q2).wait_recv()
        n = (z + 8 - STEPS[k]) % 8
        rows = from_blocks(retb[pl.ds(n * 32, 32)])
        slots = jnp.concatenate([idx_ref[pl.ds(2 * n, 1), :], idx_ref[pl.ds(2 * n + 1, 1), :]], axis=1)
        slots = jnp.broadcast_to(slots, (256, 256))
        line = lax.broadcasted_iota(jnp.int32, (256, 256), 0)

        def add(c, carry):
            at = pl.ds(pl.multiple_of(c * 256, 256), 256)
            hot = jnp.where(slots == line + 256 * c, 1.0, 0.0).astype(BF16)
            total[at, :] += dot(hot, rows)
            return carry

        lax.fori_loop(0, 8, add, 0)

    def shares(n, sem, dst):
        return pltpu.make_async_remote_copy(
            dst.at[pl.ds(0, n)], dst.at[pl.ds(0, n)], sr.at[sem], qr.at[sem], device_id=(g, j), device_id_type=MESH
        )

    shares(7, 0, r1buf).wait_recv()
    r1sum[...] = r1buf[0]
    for h in range(1, 8):
        r1sum[...] += r1buf[h]

    def send_tile(t, carry):
        @pl.when(t != j)
        def _():
            pltpu.make_async_remote_copy(
                r1sum.at[t], r2buf.at[j], sr.at[1], qr.at[1], device_id=(g, t), device_id_type=MESH
            ).start()

        return carry

    lax.fori_loop(0, PARTS, send_tile, 0)

    settle(0)
    settle(1)

    @pl.when(j < PARTS)
    def _():
        r2buf[j] = r1sum[j]
        shares(31, 1, r2buf).wait_recv()
        acc = r2buf[0]
        for t in range(1, 32):
            acc = acc + r2buf[t]
        tiles[j] = acc

        def send_sum(t, carry):
            i = (j + t) % 32
            pltpu.make_async_remote_copy(
                tiles.at[j], tiles.at[j], sr.at[2], qr.at[2], device_id=(g, i), device_id_type=MESH
            ).start()
            return carry

        lax.fori_loop(1, 32, send_sum, 0)

    settle(2)
    settle(3)

    @pl.when(j < PARTS)
    def _():
        shares(PARTS - 1, 2, tiles).wait_recv()

    @pl.when(j >= PARTS)
    def _():
        shares(PARTS, 2, tiles).wait_recv()

    def send_all(t, carry):
        h = (g + t) % 8
        pltpu.make_async_remote_copy(
            tiles.at[pl.ds(0, 16)], fin.at[g], sr.at[3], qr.at[3], device_id=(h, j), device_id_type=MESH
        ).start()
        return carry

    lax.fori_loop(1, 8, send_all, 0)
    fin[g] = tiles[pl.ds(0, 16)]

    settle(4)
    settle(5)
    settle(6)
    own2.wait()
    settle(7)

    gfv[...] = total[...].astype(BF16)
    store_gf = pltpu.make_async_copy(gfv, gf_hbm, lsem.at[6])
    store_gf.start()

    factor = 1.0 / math.sqrt(ROWS * 256)
    shares(7, 3, fin).wait_recv()
    for h in range(8):
        ref = gs_ref if h < 4 else gn_ref
        for a in range(8):
            r = (h % 4) * 64 + a * 8
            ref[r : r + 8, :128] = fin[h, 2 * a] * factor
            ref[r : r + 8, 128:] = fin[h, 2 * a + 1] * factor
    gb_ref[:, :128] = tiles[16, 0:1] * factor
    gb_ref[:, 128:] = tiles[16, 1:2] * factor

    for k in range(8):
        plane(k, outb, halob, s1, q1).wait_send()
        plane(k, outg, retb, s2, q2).wait_send()
    shares(7, 0, r1buf).wait_send()

    @pl.when(j < PARTS)
    def _():
        shares(PARTS - 1, 1, r2buf).wait_send()
        shares(31, 2, r2buf).wait_send()

    @pl.when(j >= PARTS)
    def _():
        shares(PARTS, 1, r2buf).wait_send()

    shares(7, 3, fin).wait_send()
    store_out.wait()
    store_gf.wait()


def local(
    features, w_self, w_neigh, node_bias, grad_out, send_rows, send_count, adjacency, tile_source
):
    slot_rows = send_rows[0]
    keep = lax.broadcasted_iota(jnp.int32, slot_rows.shape, 2) < send_count[0][:, :, None]
    idx = jnp.where(keep, slot_rows, -1).reshape(16, 128)
    vmem, hbm = pl.BlockSpec(memory_space=pltpu.VMEM), pl.BlockSpec(memory_space=pl.ANY)
    tall = (ROWS, WIDTH)
    blocks = (256, 16, 128)
    dma = pltpu.SemaphoreType.DMA
    out, gf, gs, gn, gb = pl.pallas_call(
        kernel,
        out_shape=(
            jax.ShapeDtypeStruct(tall, BF16),
            jax.ShapeDtypeStruct(tall, BF16),
            jax.ShapeDtypeStruct((WIDTH, WIDTH), F32),
            jax.ShapeDtypeStruct((WIDTH, WIDTH), F32),
            jax.ShapeDtypeStruct((1, WIDTH), F32),
        ),
        in_specs=[vmem, pl.BlockSpec(memory_space=pltpu.SMEM), vmem, vmem, vmem, hbm, hbm, hbm],
        out_specs=(hbm, hbm, vmem, vmem, vmem),
        scratch_shapes=[
            pltpu.VMEM((TILES, EDGE, WIDTH), BF16),
            pltpu.VMEM(tall, BF16),
            pltpu.VMEM((TILES, 2, EDGE, EDGE), jnp.int32),
            pltpu.VMEM((16, 128, 128), jnp.int32),
            pltpu.VMEM(blocks, BF16),
            pltpu.VMEM(blocks, BF16),
            pltpu.VMEM(blocks, BF16),
            pltpu.VMEM(blocks, BF16),
            pltpu.VMEM((TILES, EDGE, WIDTH), BF16),
            pltpu.VMEM((TILES, EDGE, EDGE), BF16),
            pltpu.VMEM((ROWS, ROWS), BF16),
            pltpu.VMEM((ROWS, ROWS), BF16),
            pltpu.VMEM((ROWS, EDGE), F32),
            pltpu.VMEM(tall, F32),
            pltpu.VMEM(tall, F32),
            pltpu.VMEM(tall, BF16),
            pltpu.VMEM(tall, BF16),
            pltpu.VMEM(tall, BF16),
            pltpu.VMEM(tall, F32),
            pltpu.VMEM(tall, BF16),
            pltpu.VMEM(tall, BF16),
            pltpu.VMEM((8, PARTS, 8, 128), F32),
            pltpu.VMEM((8, PARTS, 8, 128), F32),
            pltpu.VMEM((PARTS, 8, 128), F32),
            pltpu.VMEM((32, 8, 128), F32),
            pltpu.VMEM((PARTS, 8, 128), F32),
            pltpu.VMEM((8, 16, 8, 128), F32),
            dma((7,)),
            dma((8,)),
            dma((8,)),
            dma((8,)),
            dma((8,)),
            dma((4,)),
            dma((4,)),
        ],
        compiler_params=pltpu.CompilerParams(
            collective_id=0, has_side_effects=True, vmem_limit_bytes=56 << 20
        ),
        name="sage_layer",
    )(
        idx, tile_source[0], node_bias.reshape(1, WIDTH), w_self, w_neigh, features.reshape(TILES, EDGE, WIDTH), grad_out, adjacency[0]
    )
    return out, gf, gs, gn, gb.reshape(WIDTH)


def solution(mesh):
    rows = P(("group", "inner"), None)
    placed = (
        rows,
        P(),
        P(),
        P(),
        rows,
        P(("group", "inner"), None, None, None),
        P(("group", "inner"), None, None),
        P(("group", "inner"), None, None, None, None),
        P(("group", "inner"), None, None),
    )
    return jax.shard_map(
        local, mesh=mesh, in_specs=placed, out_specs=(rows, rows, P(), P(), P()), check_vma=False
    )
```

```python
import math

import jax
import jax.numpy as jnp
from jax import lax
from jax.experimental import pallas as pl
from jax.experimental.pallas import tpu as pltpu
from jax.sharding import PartitionSpec as P

MESH = pl.DeviceIdType.MESH
BF16, F32 = jnp.bfloat16, jnp.float32
ROWS, WIDTH, EDGE, TILES = 2048, 256, 128, 16
PARTS = 17
STEPS = (4, 3, 5, 2, 6, 1, 7, 0)


def dot(left, right):
    return jnp.dot(left, right, preferred_element_type=F32)


def dot_rows(left, right):
    return lax.dot_general(left, right, (((0,), (0,)), ((), ())), preferred_element_type=F32)


def dot_cols(left, right):
    return lax.dot_general(left, right, (((1,), (1,)), ((), ())), preferred_element_type=F32)


def to_blocks(rows):
    left = rows[:, :128].reshape(32, 8, 128)
    right = rows[:, 128:].reshape(32, 8, 128)
    return jnp.concatenate([left, right], axis=1).astype(BF16)


def from_blocks(blocks):
    wide = blocks.astype(F32)
    rows = jnp.concatenate([wide[:, :8], wide[:, 8:]], axis=2)
    return rows.reshape(256, 256).astype(BF16)


def kernel(
    slots_ref, count_ref, ts_ref, bias_ref, ws_ref, wn_ref, feat_hbm, gout_hbm, adj_hbm,
    out_hbm, gf_hbm, gs_ref, gn_ref, gb_ref,
    feat, gout, adj, col, outb, halob, outg, retb, halo, adj1, at_own, at_halo, inv,
    s_own, p_self, mean, gpre, gagg, total, outv, gfv,
    oht, lanes, part, r1buf, r1sum, r2buf, tiles, fin,
    lsem, s1, q1, s2, q2, sr, qr,
):
    g, j = lax.axis_index("group"), lax.axis_index("inner")
    z, y, cx, cc = j // 4, j % 4, g // 2, g % 2
    me = j * 8 + g

    load_feat = pltpu.make_async_copy(feat_hbm, feat, lsem.at[0])
    load_adj = pltpu.make_async_copy(adj_hbm, adj, lsem.at[1])
    load_gout = pltpu.make_async_copy(gout_hbm, gout, lsem.at[2])
    load_feat.start()
    load_adj.start()
    load_gout.start()

    barrier = pltpu.get_barrier_semaphore()

    def greet(t, carry):
        d = lax.rem(me + t, 256)
        pl.semaphore_signal(barrier, inc=1, device_id=(d % 8, d // 8), device_id_type=MESH)
        return carry

    lax.fori_loop(1, 256, greet, 0)

    live = lax.broadcasted_iota(jnp.int32, (8, 8, 32), 1) < count_ref[...][:, None, :]
    index = jnp.where(live, slots_ref[...], -1).reshape(64, 32)
    for i in range(32):
        col[i] = jnp.broadcast_to(index[:, i : i + 1], (64, 128)).astype(jnp.int16)
    turned = jnp.transpose(index)
    for n in range(16):
        lanes[n : n + 1, :] = jnp.concatenate([turned[2 * n : 2 * n + 1], turned[2 * n + 1 : 2 * n + 2]], axis=1)
    load_feat.wait()

    def pick(k):
        n = (z + STEPS[k]) % 8
        slab = col[pl.ds(4 * n, 4)].reshape(256, 128)
        lane = lax.broadcasted_iota(jnp.int32, (256, 128), 1)
        acc = jnp.zeros((256, 256), F32)
        for c in range(8):
            halves = [slab == (lane + 256 * c + 128 * u).astype(jnp.int16) for u in range(2)]
            hot = jnp.concatenate([jnp.where(half, BF16(1), BF16(0)) for half in halves], axis=1)
            acc = acc + dot(hot, feat[2 * c : 2 * c + 2].reshape(256, 256))
        outb[pl.ds(n * 32, 32)] = to_blocks(acc)

    pick(0)
    pl.semaphore_wait(barrier, 255)

    def send_plane(k, src, dst, ssem, rsem):
        dz = STEPS[k]

        def send(m, carry):
            h = ((cx + m // 8) % 4) * 2 + (cc + m // 4) % 2
            i = ((z + dz) % 8) * 4 + (y + m) % 4
            pltpu.make_async_remote_copy(
                src.at[i * 8 + h], dst.at[me], ssem.at[k], rsem.at[k], device_id=(h, i), device_id_type=MESH
            ).start()
            return carry

        lax.fori_loop(1 if dz == 0 else 0, 32, send, 0)

    def plane(k, src, dst, ssem, rsem):
        n = 31 if STEPS[k] == 0 else 32
        return pltpu.make_async_remote_copy(
            src.at[pl.ds(0, n)], dst.at[pl.ds(0, n)], ssem.at[k], rsem.at[k], device_id=(g, j), device_id_type=MESH
        )

    for k in range(8):
        if k:
            pick(k)
        send_plane(k, outb, halob, s1, q1)
    own1 = pltpu.make_async_copy(outb.at[me], halob.at[me], lsem.at[3])
    own1.start()

    load_adj.wait()

    def prepare(b, carry):
        rows = pl.ds(pl.multiple_of(b * EDGE, EDGE), EDGE)
        a0 = adj[b, 0].astype(F32)
        a1 = adj[b, 1].astype(F32)
        degree = jnp.sum(a0 + a1, axis=1, keepdims=True)
        inv[rows, :] = jnp.broadcast_to(1.0 / jnp.maximum(degree, 1.0), (EDGE, EDGE))
        adj1[b] = a1.astype(BF16)
        t0 = ts_ref[0, b]
        t1 = jnp.maximum(ts_ref[1, b] - TILES, 0)
        block = feat[t0]
        s_own[rows, :] = dot(a0.astype(BF16), block)
        p_self[rows, :] = dot(feat[b], ws_ref[...]) + bias_ref[...]
        a0t = jnp.transpose(a0)
        a1t = jnp.transpose(a1)
        own = jnp.broadcast_to(t0, (EDGE, EDGE))
        far = jnp.broadcast_to(t1, (EDGE, EDGE))
        for e in range(TILES):
            at_own[e * EDGE : (e + 1) * EDGE, rows] = jnp.where(own == e, a0t, 0.0).astype(BF16)
            at_halo[e * EDGE : (e + 1) * EDGE, rows] = jnp.where(far == e, a1t, 0.0).astype(BF16)
        return carry

    lax.fori_loop(0, TILES, prepare, 0)

    def spread(n, carry):
        slots = jnp.concatenate([lanes[pl.ds(2 * n, 1), :], lanes[pl.ds(2 * n + 1, 1), :]], axis=1)
        line = lax.broadcasted_iota(jnp.int32, (256, 256), 0).astype(jnp.int16)
        for c in range(8):
            here = jnp.broadcast_to(slots - 256 * c, (256, 256)).astype(jnp.int16)
            hot = jnp.where(here == line, BF16(1), BF16(0))
            oht[256 * c : 256 * c + 256, pl.ds(pl.multiple_of(n * 256, 256), 256)] = hot
        return carry

    lax.fori_loop(0, 8, spread, 0)
    load_gout.wait()

    own1.wait()
    for k in range(8):
        plane(k, outb, halob, s1, q1).wait_recv()
        n = (z + 8 - STEPS[k]) % 8
        halo[pl.ds(2 * n, 2)] = from_blocks(halob[pl.ds(n * 32, 32)]).reshape(2, EDGE, WIDTH)

    def layer(b, carry):
        rows = pl.ds(pl.multiple_of(b * 256, 256), 256)
        sums = []
        for u in range(2):
            t1 = jnp.maximum(ts_ref[1, 2 * b + u] - TILES, 0)
            block = halo[t1]
            sums.append(dot(adj1[2 * b + u], block))
        scale = inv[rows, :]
        scale = jnp.concatenate([scale, scale], axis=1)
        m = ((s_own[rows, :] + jnp.concatenate(sums, axis=0)) * scale).astype(BF16)
        mean[rows, :] = m
        pre = p_self[rows, :] + dot(m, wn_ref[...])
        sigma = 1.0 / (1.0 + jnp.exp(-pre))
        outv[rows, :] = (pre * sigma).astype(BF16)
        slope = sigma * (1.0 + pre * (1.0 - sigma))
        gp = (gout[rows, :].astype(F32) * slope).astype(BF16)
        gpre[rows, :] = gp
        gagg[rows, :] = (dot_cols(gp, wn_ref[...]) * scale).astype(BF16)
        return carry

    lax.fori_loop(0, 8, layer, 0, unroll=2)
    store_out = pltpu.make_async_copy(outv, out_hbm, lsem.at[4])
    store_out.start()

    def give_back(k):
        n = (z + STEPS[k]) % 8
        rows = pl.ds(pl.multiple_of(n * 256, 256), 256)
        acc = jnp.zeros((256, 256), F32)
        for c in range(8):
            acc = acc + dot(at_halo[rows, 256 * c : 256 * c + 256], gagg[256 * c : 256 * c + 256, :])
        outg[pl.ds(n * 32, 32)] = to_blocks(acc)
        send_plane(k, outg, retb, s2, q2)

    for k in range(3):
        give_back(k)

    def weights(c, carry):
        acc_self, acc_neigh, acc_bias = carry
        rows = pl.ds(pl.multiple_of(c * 256, 256), 256)
        gp = gpre[rows, :]
        acc_self = acc_self + dot_rows(feat[pl.ds(2 * c, 2)].reshape(256, 256), gp)
        acc_neigh = acc_neigh + dot_rows(mean[rows, :], gp)
        acc_bias = acc_bias + jnp.sum(gp.astype(F32).reshape(32, 8, 256), axis=0)
        return acc_self, acc_neigh, acc_bias

    zero = jnp.zeros((256, 256), F32)
    acc_self, acc_neigh, acc_bias = lax.fori_loop(0, 8, weights, (zero, zero, jnp.zeros((8, 256), F32)))
    bias_row = jnp.sum(acc_bias, axis=0, keepdims=True)
    bias_tile = jnp.concatenate([bias_row[:, :128], bias_row[:, 128:], jnp.zeros((6, 128), F32)], axis=0)
    for h in range(8):
        acc = acc_self if h < 4 else acc_neigh
        for a in range(8):
            r = (h % 4) * 64 + a * 8
            part[h, 2 * a] = acc[r : r + 8, :128]
            part[h, 2 * a + 1] = acc[r : r + 8, 128:]
        part[h, 16] = bias_tile

    def send_share(t, carry):
        h = (g + t) % 8
        pltpu.make_async_remote_copy(
            part.at[h], r1buf.at[g], sr.at[0], qr.at[0], device_id=(h, j), device_id_type=MESH
        ).start()
        return carry

    lax.fori_loop(1, 8, send_share, 0)
    r1buf[g] = part[g]

    for k in range(3, 8):
        give_back(k)
    own2 = pltpu.make_async_copy(outg.at[me], retb.at[me], lsem.at[5])
    own2.start()

    def settle(ks, last=False):
        planes, spots = [], []
        for k in ks:
            plane(k, outg, retb, s2, q2).wait_recv()
            n = (z + 8 - STEPS[k]) % 8
            planes.append(from_blocks(retb[pl.ds(n * 32, 32)]))
            spots.append(pl.ds(pl.multiple_of(n * 256, 256), 256))
        for c in range(8):
            at = slice(256 * c, 256 * c + 256)
            acc = total[at, :]
            for spot, rows in zip(spots, planes):
                acc = acc + dot(oht[at, spot], rows)
            if last:
                gfv[at, :] = acc.astype(BF16)
            else:
                total[at, :] = acc

    def shares(n, sem, dst):
        return pltpu.make_async_remote_copy(
            dst.at[pl.ds(0, n)], dst.at[pl.ds(0, n)], sr.at[sem], qr.at[sem], device_id=(g, j), device_id_type=MESH
        )

    shares(7, 0, r1buf).wait_recv()
    r1sum[...] = r1buf[0]
    for h in range(1, 8):
        r1sum[...] += r1buf[h]

    def send_tile(t, carry):
        @pl.when(t != j)
        def _():
            pltpu.make_async_remote_copy(
                r1sum.at[t], r2buf.at[j], sr.at[1], qr.at[1], device_id=(g, t), device_id_type=MESH
            ).start()

        return carry

    lax.fori_loop(0, PARTS, send_tile, 0)

    def base(n, carry):
        rows = pl.ds(pl.multiple_of(n * 256, 256), 256)
        acc = dot_cols(gpre[rows, :], ws_ref[...])
        for c in range(8):
            acc = acc + dot(at_own[rows, 256 * c : 256 * c + 256], gagg[256 * c : 256 * c + 256, :])
        total[rows, :] = acc
        return carry

    lax.fori_loop(0, 8, base, 0)


    @pl.when(j < PARTS)
    def _():
        r2buf[j] = r1sum[j]
        shares(31, 1, r2buf).wait_recv()
        acc = r2buf[0]
        for t in range(1, 32):
            acc = acc + r2buf[t]
        tiles[j] = acc

        def send_sum(t, carry):
            i = (j + t) % 32
            pltpu.make_async_remote_copy(
                tiles.at[j], tiles.at[j], sr.at[2], qr.at[2], device_id=(g, i), device_id_type=MESH
            ).start()
            return carry

        lax.fori_loop(1, 32, send_sum, 0)

    settle((0,))
    settle((1, 2))

    @pl.when(j < PARTS)
    def _():
        shares(PARTS - 1, 2, tiles).wait_recv()

    @pl.when(j >= PARTS)
    def _():
        shares(PARTS, 2, tiles).wait_recv()

    def send_all(t, carry):
        h = (g + t) % 8
        pltpu.make_async_remote_copy(
            tiles.at[pl.ds(0, 16)], fin.at[g], sr.at[3], qr.at[3], device_id=(h, j), device_id_type=MESH
        ).start()
        return carry

    lax.fori_loop(1, 8, send_all, 0)
    fin[g] = tiles[pl.ds(0, 16)]

    settle((3, 4))
    settle((5, 6))
    own2.wait()
    settle((7,), True)
    store_gf = pltpu.make_async_copy(gfv, gf_hbm, lsem.at[6])
    store_gf.start()

    factor = 1.0 / math.sqrt(ROWS * 256)
    shares(7, 3, fin).wait_recv()
    for h in range(8):
        ref = gs_ref if h < 4 else gn_ref
        for a in range(8):
            r = (h % 4) * 64 + a * 8
            ref[r : r + 8, :128] = fin[h, 2 * a] * factor
            ref[r : r + 8, 128:] = fin[h, 2 * a + 1] * factor
    gb_ref[:, :128] = tiles[16, 0:1] * factor
    gb_ref[:, 128:] = tiles[16, 1:2] * factor

    for k in range(8):
        plane(k, outb, halob, s1, q1).wait_send()
        plane(k, outg, retb, s2, q2).wait_send()
    shares(7, 0, r1buf).wait_send()

    @pl.when(j < PARTS)
    def _():
        shares(PARTS - 1, 1, r2buf).wait_send()
        shares(31, 2, r2buf).wait_send()

    @pl.when(j >= PARTS)
    def _():
        shares(PARTS, 1, r2buf).wait_send()

    shares(7, 3, fin).wait_send()
    store_out.wait()
    store_gf.wait()


def hand_over(*refs):
    held, sems = refs[10:15], refs[15]
    taken = [pltpu.make_async_copy(refs[n], held[n], sems.at[n]) for n in range(5)]
    given = [pltpu.make_async_copy(held[n], refs[5 + n], sems.at[5 + n]) for n in range(5)]
    for copy in taken:
        copy.start()
    for n in range(5):
        taken[n].wait()
        given[n].start()
    for copy in given:
        copy.wait()


def local(
    features, w_self, w_neigh, node_bias, grad_out, send_rows, send_count, adjacency, tile_source
):
    vmem, hbm = pl.BlockSpec(memory_space=pltpu.VMEM), pl.BlockSpec(memory_space=pl.ANY)
    tall = (ROWS, WIDTH)
    blocks = (256, 16, 128)
    dma = pltpu.SemaphoreType.DMA
    made = pl.pallas_call(
        kernel,
        out_shape=(
            jax.ShapeDtypeStruct(tall, BF16),
            jax.ShapeDtypeStruct(tall, BF16),
            jax.ShapeDtypeStruct((WIDTH, WIDTH), F32),
            jax.ShapeDtypeStruct((WIDTH, WIDTH), F32),
            jax.ShapeDtypeStruct((1, WIDTH), F32),
        ),
        in_specs=[vmem, vmem, pl.BlockSpec(memory_space=pltpu.SMEM), vmem, vmem, vmem, hbm, hbm, hbm],
        out_specs=(hbm, hbm, vmem, vmem, vmem),
        scratch_shapes=[
            pltpu.VMEM((TILES, EDGE, WIDTH), BF16),
            pltpu.VMEM(tall, BF16),
            pltpu.VMEM((TILES, 2, EDGE, EDGE), jnp.int32),
            pltpu.VMEM((32, 64, 128), jnp.int16),
            pltpu.VMEM(blocks, BF16),
            pltpu.VMEM(blocks, BF16),
            pltpu.VMEM(blocks, BF16),
            pltpu.VMEM(blocks, BF16),
            pltpu.VMEM((TILES, EDGE, WIDTH), BF16),
            pltpu.VMEM((TILES, EDGE, EDGE), BF16),
            pltpu.VMEM((ROWS, ROWS), BF16),
            pltpu.VMEM((ROWS, ROWS), BF16),
            pltpu.VMEM((ROWS, EDGE), F32),
            pltpu.VMEM(tall, F32),
            pltpu.VMEM(tall, F32),
            pltpu.VMEM(tall, BF16),
            pltpu.VMEM(tall, BF16),
            pltpu.VMEM(tall, BF16),
            pltpu.VMEM(tall, F32),
            pltpu.VMEM(tall, BF16),
            pltpu.VMEM(tall, BF16),
            pltpu.VMEM((ROWS, ROWS), BF16),
            pltpu.VMEM((16, 128), jnp.int32),
            pltpu.VMEM((8, PARTS, 8, 128), F32),
            pltpu.VMEM((8, PARTS, 8, 128), F32),
            pltpu.VMEM((PARTS, 8, 128), F32),
            pltpu.VMEM((32, 8, 128), F32),
            pltpu.VMEM((PARTS, 8, 128), F32),
            pltpu.VMEM((8, 16, 8, 128), F32),
            dma((7,)),
            dma((8,)),
            dma((8,)),
            dma((8,)),
            dma((8,)),
            dma((4,)),
            dma((4,)),
        ],
        compiler_params=pltpu.CompilerParams(
            collective_id=0, has_side_effects=True, vmem_limit_bytes=56 << 20
        ),
        name="sage_layer",
    )(
        send_rows[0].transpose(1, 2, 0), send_count[0].T, tile_source[0].T, node_bias.reshape(1, WIDTH), w_self, w_neigh, features.reshape(TILES, EDGE, WIDTH), grad_out, adjacency[0]
    )
    out, gf, gs, gn, gb = pl.pallas_call(
        hand_over,
        out_shape=[jax.ShapeDtypeStruct(a.shape, a.dtype) for a in made],
        in_specs=[hbm] * 5,
        out_specs=[hbm] * 5,
        scratch_shapes=[pltpu.VMEM(a.shape, a.dtype) for a in made] + [dma((10,))],
        compiler_params=pltpu.CompilerParams(vmem_limit_bytes=60 << 20),
        name="hand_over",
    )(*made)
    return out, gf, gs, gn, gb.reshape(WIDTH)


def solution(mesh):
    rows = P(("group", "inner"), None)
    placed = (
        rows,
        P(),
        P(),
        P(),
        rows,
        P(("group", "inner"), None, None, None),
        P(("group", "inner"), None, None),
        P(("group", "inner"), None, None, None, None),
        P(("group", "inner"), None, None),
    )
    return jax.shard_map(
        local, mesh=mesh, in_specs=placed, out_specs=(rows, rows, P(), P(), P()), check_vma=False
    )
```

```python
import math

import jax
import jax.numpy as jnp
from jax import lax
from jax.experimental import pallas as pl
from jax.experimental.pallas import tpu as pltpu
from jax.sharding import PartitionSpec as P

FLAT = pl.DeviceIdType.LOGICAL
BF16, F32 = jnp.bfloat16, jnp.float32
ROWS, WIDTH, EDGE, TILES = 2048, 256, 128, 16
OWNERS = 32
ROUNDS = ((4,), (3, 5), (2, 6), (1, 7), (0,))


def dot(left, right):
    return jnp.dot(left, right, preferred_element_type=F32)


def dot_rows(left, right):
    return lax.dot_general(left, right, (((0,), (0,)), ((), ())), preferred_element_type=F32)


def dot_cols(left, right):
    return lax.dot_general(left, right, (((1,), (1,)), ((), ())), preferred_element_type=F32)


def to_blocks(rows):
    left = rows[:, :128].reshape(32, 8, 128)
    right = rows[:, 128:].reshape(32, 8, 128)
    return jnp.concatenate([left, right], axis=1).astype(BF16)


def from_blocks(blocks):
    wide = blocks.astype(F32)
    rows = jnp.concatenate([wide[:, :8], wide[:, 8:]], axis=2)
    return rows.reshape(256, 256).astype(BF16)


def kernel(
    slots_ref, count_ref, ts_ref, bias_ref, ws_ref, wn_ref, feat_hbm, gout_hbm, adj_hbm,
    out_ref, gf_ref, gs_ref, gn_ref, gb_ref,
    feat, gout, adj, col, outb, halob, outg, retb, halo, adj1, at_own, at_halo, inv,
    s_own, p_self, mean, gpre, gagg, total,
    oht, lanes, part, shares, layers, done, b_shares, b_layers, b_done,
    lsem, s1, q1, s2, q2, sr, qr,
):
    g, j = lax.axis_index("group"), lax.axis_index("inner")
    z, y, cx, cc = j // 4, j % 4, g // 2, g % 2
    me, flat = j * 8 + g, g * 32 + j

    load_feat = pltpu.make_async_copy(feat_hbm, feat, lsem.at[0])
    load_adj = pltpu.make_async_copy(adj_hbm, adj, lsem.at[1])
    load_gout = pltpu.make_async_copy(gout_hbm, gout, lsem.at[2])
    load_feat.start()
    load_adj.start()
    load_gout.start()

    barrier = pltpu.get_barrier_semaphore()

    def greet(t, carry):
        d = lax.rem(flat + t, 256)
        pl.semaphore_signal(barrier, inc=1, device_id=d, device_id_type=FLAT)
        return carry

    lax.fori_loop(1, 256, greet, 0, unroll=5)

    live = lax.broadcasted_iota(jnp.int32, (8, 8, 32), 1) < count_ref[...][:, None, :]
    index = jnp.where(live, slots_ref[...], -1).reshape(64, 32)
    for i in range(32):
        col[i] = jnp.broadcast_to(index[:, i : i + 1], (64, 128)).astype(jnp.int16)
    turned = jnp.transpose(index)
    for n in range(16):
        lanes[n : n + 1, :] = jnp.concatenate([turned[2 * n : 2 * n + 1], turned[2 * n + 1 : 2 * n + 2]], axis=1)
    load_feat.wait()

    def pick(dz):
        n = (z + dz) % 8
        slab = col[pl.ds(4 * n, 4)].reshape(256, 128)
        lane = lax.broadcasted_iota(jnp.int32, (256, 128), 1)
        acc = jnp.zeros((256, 256), F32)
        for c in range(8):
            halves = [slab == (lane + 256 * c + 128 * u).astype(jnp.int16) for u in range(2)]
            hot = jnp.concatenate([jnp.where(half, BF16(1), BF16(0)) for half in halves], axis=1)
            acc = acc + dot(hot, feat[2 * c : 2 * c + 2].reshape(256, 256))
        outb[pl.ds(n * 32, 32)] = to_blocks(acc)

    pick(ROUNDS[0][0])
    pl.semaphore_wait(barrier, 255)

    def send_round(steps, src, dst, ssem, rsem):
        def send(m, carry):
            h = ((cx + m // 8) % 4) * 2 + (cc + m // 4) % 2
            for dz in steps:
                i = ((z + dz) % 8) * 4 + (y + m) % 4
                pltpu.make_async_remote_copy(
                    src.at[i * 8 + h], dst.at[me], ssem.at[dz], rsem.at[dz], device_id=h * 32 + i, device_id_type=FLAT
                ).start()
            return carry

        if steps[0] == 0:
            lax.fori_loop(1, 32, send, 0)
        else:
            lax.fori_loop(0, 32, send, 0, unroll=2)

    def plane(dz, src, dst, ssem, rsem):
        n = 32 if dz else 31
        return pltpu.make_async_remote_copy(
            src.at[pl.ds(0, n)], dst.at[pl.ds(0, n)], ssem.at[dz], rsem.at[dz], device_id=flat, device_id_type=FLAT
        )

    for steps in ROUNDS:
        for dz in steps:
            if dz != ROUNDS[0][0]:
                pick(dz)
        send_round(steps, outb, halob, s1, q1)
    own1 = pltpu.make_async_copy(outb.at[me], halob.at[me], lsem.at[3])
    own1.start()

    load_adj.wait()

    def prepare(b, carry):
        rows = pl.ds(pl.multiple_of(b * EDGE, EDGE), EDGE)
        a0 = adj[b, 0].astype(F32)
        a1 = adj[b, 1].astype(F32)
        degree = jnp.sum(a0 + a1, axis=1, keepdims=True)
        inv[rows, :] = jnp.broadcast_to(1.0 / jnp.maximum(degree, 1.0), (EDGE, EDGE))
        adj1[b] = a1.astype(BF16)
        t0 = ts_ref[0, b]
        t1 = jnp.maximum(ts_ref[1, b] - TILES, 0)
        block = feat[t0]
        s_own[rows, :] = dot(a0.astype(BF16), block)
        p_self[rows, :] = dot(feat[b], ws_ref[...]) + bias_ref[...]
        a0t = jnp.transpose(a0)
        a1t = jnp.transpose(a1)
        own = jnp.broadcast_to(t0, (EDGE, EDGE))
        far = jnp.broadcast_to(t1, (EDGE, EDGE))
        for e in range(TILES):
            at_own[e * EDGE : (e + 1) * EDGE, rows] = jnp.where(own == e, a0t, 0.0).astype(BF16)
            at_halo[e * EDGE : (e + 1) * EDGE, rows] = jnp.where(far == e, a1t, 0.0).astype(BF16)
        return carry

    lax.fori_loop(0, TILES, prepare, 0)

    def spread(n, carry):
        slots = jnp.concatenate([lanes[pl.ds(2 * n, 1), :], lanes[pl.ds(2 * n + 1, 1), :]], axis=1)
        line = lax.broadcasted_iota(jnp.int32, (256, 256), 0).astype(jnp.int16)
        for c in range(8):
            here = jnp.broadcast_to(slots - 256 * c, (256, 256)).astype(jnp.int16)
            hot = jnp.where(here == line, BF16(1), BF16(0))
            oht[256 * c : 256 * c + 256, pl.ds(pl.multiple_of(n * 256, 256), 256)] = hot
        return carry

    lax.fori_loop(0, 8, spread, 0)
    load_gout.wait()

    own1.wait()
    for steps in ROUNDS:
        for dz in steps:
            plane(dz, outb, halob, s1, q1).wait_recv()
            n = (z + 8 - dz) % 8
            halo[pl.ds(2 * n, 2)] = from_blocks(halob[pl.ds(n * 32, 32)]).reshape(2, EDGE, WIDTH)

    def layer(b, carry):
        rows = pl.ds(pl.multiple_of(b * 256, 256), 256)
        sums = []
        for u in range(2):
            t1 = jnp.maximum(ts_ref[1, 2 * b + u] - TILES, 0)
            block = halo[t1]
            sums.append(dot(adj1[2 * b + u], block))
        scale = inv[rows, :]
        scale = jnp.concatenate([scale, scale], axis=1)
        m = ((s_own[rows, :] + jnp.concatenate(sums, axis=0)) * scale).astype(BF16)
        mean[rows, :] = m
        pre = p_self[rows, :] + dot(m, wn_ref[...])
        sigma = 0.5 + 0.5 * jnp.tanh(0.5 * pre)
        out_ref[rows, :] = (pre * sigma).astype(BF16)
        slope = sigma * (1.0 + pre * (1.0 - sigma))
        gp = (gout[rows, :].astype(F32) * slope).astype(BF16)
        gpre[rows, :] = gp
        gagg[rows, :] = (dot_cols(gp, wn_ref[...]) * scale).astype(BF16)
        return carry

    lax.fori_loop(0, 8, layer, 0, unroll=4)

    def give_back(steps):
        for dz in steps:
            n = (z + dz) % 8
            rows = pl.ds(pl.multiple_of(n * 256, 256), 256)
            acc = jnp.zeros((256, 256), F32)
            for c in range(8):
                acc = acc + dot(at_halo[rows, 256 * c : 256 * c + 256], gagg[256 * c : 256 * c + 256, :])
            outg[pl.ds(n * 32, 32)] = to_blocks(acc)
        send_round(steps, outg, retb, s2, q2)

    give_back(ROUNDS[0])
    give_back(ROUNDS[1])

    def weights(c, carry):
        acc_self, acc_neigh, acc_bias = carry
        rows = pl.ds(pl.multiple_of(c * 256, 256), 256)
        gp = gpre[rows, :]
        acc_self = acc_self + dot_rows(feat[pl.ds(2 * c, 2)].reshape(256, 256), gp)
        acc_neigh = acc_neigh + dot_rows(mean[rows, :], gp)
        acc_bias = acc_bias + jnp.sum(gp.astype(F32).reshape(32, 8, 256), axis=0)
        return acc_self, acc_neigh, acc_bias

    zero = jnp.zeros((256, 256), F32)
    acc_self, acc_neigh, acc_bias = lax.fori_loop(0, 8, weights, (zero, zero, jnp.zeros((8, 256), F32)))
    part[0:16] = acc_self.reshape(16, 16, WIDTH)
    part[16:32] = acc_neigh.reshape(16, 16, WIDTH)
    bias_row = jnp.sum(acc_bias, axis=0, keepdims=True)

    spot = g * 4 + y
    b_shares[spot] = jnp.concatenate([bias_row[:, :128], bias_row[:, 128:], jnp.zeros((6, 128), F32)], axis=0)

    def send_share(t, carry):
        o = lax.rem(spot + t, OWNERS)
        pltpu.make_async_remote_copy(
            part.at[o], shares.at[spot], sr.at[0], qr.at[0], device_id=(o // 4) * 32 + z * 4 + o % 4, device_id_type=FLAT
        ).start()
        return carry

    lax.fori_loop(1, OWNERS, send_share, 0)
    shares[spot] = part[spot]

    @pl.when(spot != 0)
    def _():
        pltpu.make_async_remote_copy(
            b_shares.at[spot], b_shares.at[spot], sr.at[3], qr.at[3], device_id=z * 4, device_id_type=FLAT
        ).start()

    give_back(ROUNDS[2])
    give_back(ROUNDS[3])
    give_back(ROUNDS[4])
    own2 = pltpu.make_async_copy(outg.at[me], retb.at[me], lsem.at[5])
    own2.start()

    def batch(n, sem, dst):
        return pltpu.make_async_remote_copy(
            dst.at[pl.ds(0, n)], dst.at[pl.ds(0, n)], sr.at[sem], qr.at[sem], device_id=flat, device_id_type=FLAT
        )

    batch(31, 0, shares).wait_recv()
    acc = shares[0]
    for o in range(1, OWNERS):
        acc = acc + shares[o]
    layers[z] = acc

    def send_layer(t, carry):
        to = lax.rem(z + t, 8)
        pltpu.make_async_remote_copy(
            layers.at[z], layers.at[z], sr.at[1], qr.at[1], device_id=g * 32 + to * 4 + y, device_id_type=FLAT
        ).start()
        return carry

    lax.fori_loop(1, 8, send_layer, 0)

    @pl.when(spot == 0)
    def _():
        batch(31, 3, b_shares).wait_recv()
        total_bias = b_shares[0]
        for o in range(1, OWNERS):
            total_bias = total_bias + b_shares[o]
        b_layers[z] = total_bias

        def send_bias(t, carry):
            to = lax.rem(z + t, 8)
            pltpu.make_async_remote_copy(
                b_layers.at[z], b_layers.at[z], sr.at[4], qr.at[4], device_id=to * 4, device_id_type=FLAT
            ).start()
            return carry

        lax.fori_loop(1, 8, send_bias, 0)

    def settle(steps, last=False):
        planes, spots = [], []
        for dz in steps:
            plane(dz, outg, retb, s2, q2).wait_recv()
            n = (z + 8 - dz) % 8
            planes.append(from_blocks(retb[pl.ds(n * 32, 32)]))
            spots.append(pl.ds(pl.multiple_of(n * 256, 256), 256))
        for c in range(8):
            at = slice(256 * c, 256 * c + 256)
            acc = total[at, :]
            for place, rows in zip(spots, planes):
                acc = acc + dot(oht[at, place], rows)
            if last:
                gf_ref[at, :] = acc.astype(BF16)
            else:
                total[at, :] = acc

    def base(n, carry):
        rows = pl.ds(pl.multiple_of(n * 256, 256), 256)
        acc = dot_cols(gpre[rows, :], ws_ref[...])
        for c in range(8):
            acc = acc + dot(at_own[rows, 256 * c : 256 * c + 256], gagg[256 * c : 256 * c + 256, :])
        total[rows, :] = acc
        return carry

    lax.fori_loop(0, 8, base, 0)

    batch(7, 1, layers).wait_recv()
    acc = layers[0]
    for k in range(1, 8):
        acc = acc + layers[k]
    factor = 1.0 / math.sqrt(ROWS * 256)
    done[spot] = (acc * factor).astype(done.dtype)

    def send_done(t, carry):
        o = lax.rem(spot + t, OWNERS)
        pltpu.make_async_remote_copy(
            done.at[spot], done.at[spot], sr.at[2], qr.at[2], device_id=(o // 4) * 32 + z * 4 + o % 4, device_id_type=FLAT
        ).start()
        return carry

    lax.fori_loop(1, OWNERS, send_done, 0)

    @pl.when(spot == 0)
    def _():
        batch(7, 4, b_layers).wait_recv()
        total_bias = b_layers[0]
        for k in range(1, 8):
            total_bias = total_bias + b_layers[k]
        b_done[0] = total_bias * factor

        def send_bias(o, carry):
            pltpu.make_async_remote_copy(
                b_done.at[0], b_done.at[0], sr.at[5], qr.at[5], device_id=(o // 4) * 32 + z * 4 + o % 4, device_id_type=FLAT
            ).start()
            return carry

        lax.fori_loop(1, OWNERS, send_bias, 0)

    settle(ROUNDS[0])
    settle(ROUNDS[1])
    settle(ROUNDS[2])
    settle(ROUNDS[3])
    own2.wait()
    settle(ROUNDS[4], True)

    batch(31, 2, done).wait_recv()
    gs_ref[...] = done[0:16].astype(F32).reshape(WIDTH, WIDTH)
    gn_ref[...] = done[16:32].astype(F32).reshape(WIDTH, WIDTH)

    @pl.when(spot != 0)
    def _():
        batch(1, 5, b_done).wait_recv()

    gb_ref[:, :128] = b_done[0, 0:1]
    gb_ref[:, 128:] = b_done[0, 1:2]

    for dz in range(8):
        plane(dz, outb, halob, s1, q1).wait_send()
        plane(dz, outg, retb, s2, q2).wait_send()
    batch(31, 0, shares).wait_send()
    batch(7, 1, layers).wait_send()
    batch(31, 2, done).wait_send()

    @pl.when(spot != 0)
    def _():
        batch(1, 3, b_shares).wait_send()

    @pl.when(spot == 0)
    def _():
        batch(7, 4, b_layers).wait_send()
        batch(31, 5, b_shares).wait_send()


def hand_over(*refs):
    sems = refs[10]
    copies = [pltpu.make_async_copy(refs[n], refs[5 + n], sems.at[n]) for n in range(5)]
    for copy in copies:
        copy.start()
    for copy in copies:
        copy.wait()


def local(
    features, w_self, w_neigh, node_bias, grad_out, send_rows, send_count, adjacency, tile_source
):
    vmem, hbm = pl.BlockSpec(memory_space=pltpu.VMEM), pl.BlockSpec(memory_space=pl.ANY)
    tall = (ROWS, WIDTH)
    blocks = (256, 16, 128)
    dma = pltpu.SemaphoreType.DMA
    shapes = [
        jax.ShapeDtypeStruct(tall, BF16),
        jax.ShapeDtypeStruct(tall, BF16),
        jax.ShapeDtypeStruct((WIDTH, WIDTH), F32),
        jax.ShapeDtypeStruct((WIDTH, WIDTH), F32),
        jax.ShapeDtypeStruct((1, WIDTH), F32),
    ]
    made = pl.pallas_call(
        kernel,
        out_shape=[pltpu.VMEM(a.shape, a.dtype) for a in shapes],
        in_specs=[vmem, vmem, pl.BlockSpec(memory_space=pltpu.SMEM), vmem, vmem, vmem, hbm, hbm, hbm],
        out_specs=[vmem] * 5,
        scratch_shapes=[
            pltpu.VMEM((TILES, EDGE, WIDTH), BF16),
            pltpu.VMEM(tall, BF16),
            pltpu.VMEM((TILES, 2, EDGE, EDGE), jnp.int32),
            pltpu.VMEM((32, 64, 128), jnp.int16),
            pltpu.VMEM(blocks, BF16),
            pltpu.VMEM(blocks, BF16),
            pltpu.VMEM(blocks, BF16),
            pltpu.VMEM(blocks, BF16),
            pltpu.VMEM((TILES, EDGE, WIDTH), BF16),
            pltpu.VMEM((TILES, EDGE, EDGE), BF16),
            pltpu.VMEM((ROWS, ROWS), BF16),
            pltpu.VMEM((ROWS, ROWS), BF16),
            pltpu.VMEM((ROWS, EDGE), F32),
            pltpu.VMEM(tall, F32),
            pltpu.VMEM(tall, F32),
            pltpu.VMEM(tall, BF16),
            pltpu.VMEM(tall, BF16),
            pltpu.VMEM(tall, BF16),
            pltpu.VMEM(tall, F32),
            pltpu.VMEM((ROWS, ROWS), BF16),
            pltpu.VMEM((16, 128), jnp.int32),
            pltpu.VMEM((OWNERS, 16, WIDTH), F32),
            pltpu.VMEM((OWNERS, 16, WIDTH), F32),
            pltpu.VMEM((8, 16, WIDTH), F32),
            pltpu.VMEM((OWNERS, 16, WIDTH), BF16),
            pltpu.VMEM((OWNERS, 8, 128), F32),
            pltpu.VMEM((8, 8, 128), F32),
            pltpu.VMEM((1, 8, 128), F32),
            dma((7,)),
            dma((8,)),
            dma((8,)),
            dma((8,)),
            dma((8,)),
            dma((6,)),
            dma((6,)),
        ],
        compiler_params=pltpu.CompilerParams(
            collective_id=0, has_side_effects=True, vmem_limit_bytes=54 << 20
        ),
        name="sage_layer",
    )(
        send_rows[0].transpose(1, 2, 0), send_count[0].T, tile_source[0].T, node_bias.reshape(1, WIDTH), w_self, w_neigh, features.reshape(TILES, EDGE, WIDTH), grad_out, adjacency[0]
    )
    out, gf, gs, gn, gb = pl.pallas_call(
        hand_over,
        out_shape=shapes,
        in_specs=[vmem] * 5,
        out_specs=[hbm] * 5,
        scratch_shapes=[dma((5,))],
        compiler_params=pltpu.CompilerParams(vmem_limit_bytes=4 << 20),
        name="hand_over",
    )(*made)
    return out, gf, gs, gn, gb.reshape(WIDTH)


def solution(mesh):
    rows = P(("group", "inner"), None)
    placed = (
        rows,
        P(),
        P(),
        P(),
        rows,
        P(("group", "inner"), None, None, None),
        P(("group", "inner"), None, None),
        P(("group", "inner"), None, None, None, None),
        P(("group", "inner"), None, None),
    )
    return jax.shard_map(
        local, mesh=mesh, in_specs=placed, out_specs=(rows, rows, P(), P(), P()), check_vma=False
    )
```

```python
import math

import jax
import jax.numpy as jnp
from jax import lax
from jax.experimental import pallas as pl
from jax.experimental.pallas import tpu as pltpu
from jax.sharding import PartitionSpec as P

FLAT = pl.DeviceIdType.LOGICAL
BF16, F32 = jnp.bfloat16, jnp.float32
ROWS, WIDTH, EDGE, TILES = 2048, 256, 128, 16
OWNERS = 32
EARLY = 2
ROUNDS = ((4,), (3, 5), (2, 6), (1, 7), (0,))


def dot(left, right):
    return jnp.dot(left, right, preferred_element_type=F32)


def dot_rows(left, right):
    return lax.dot_general(left, right, (((0,), (0,)), ((), ())), preferred_element_type=F32)


def dot_cols(left, right):
    return lax.dot_general(left, right, (((1,), (1,)), ((), ())), preferred_element_type=F32)


def to_blocks(rows):
    left = rows[:, :128].reshape(32, 8, 128)
    right = rows[:, 128:].reshape(32, 8, 128)
    return jnp.concatenate([left, right], axis=1).astype(BF16)


def from_blocks(blocks):
    wide = blocks.astype(F32)
    rows = jnp.concatenate([wide[:, :8], wide[:, 8:]], axis=2)
    return rows.reshape(256, 256).astype(BF16)


def kernel(
    slots_ref, count_ref, ts_ref, bias_ref, ws_ref, wn_ref, feat_hbm, gout_hbm, adj_hbm,
    out_ref, gf_ref, gs_ref, gn_ref, gb_ref,
    feat, gout, adj, col, outb, halob, outg, retb, halo, adj1, at_own, at_halo, inv,
    s_own, p_self, mean, gpre, gagg, total,
    oht, lanes, part, shares, layers, done, b_shares, b_layers, b_done,
    lsem, s1, q1, s2, q2, sr, qr,
):
    g, j = lax.axis_index("group"), lax.axis_index("inner")
    z, y, cx, cc = j // 4, j % 4, g // 2, g % 2
    me, flat = j * 8 + g, g * 32 + j

    load_feat = pltpu.make_async_copy(feat_hbm, feat, lsem.at[0])
    load_adj = pltpu.make_async_copy(adj_hbm, adj, lsem.at[1])
    load_gout = pltpu.make_async_copy(gout_hbm, gout, lsem.at[2])
    load_feat.start()
    load_adj.start()
    load_gout.start()

    barrier = pltpu.get_barrier_semaphore()

    def greet(t, carry):
        d = lax.rem(flat + t, 256)
        pl.semaphore_signal(barrier, inc=1, device_id=d, device_id_type=FLAT)
        return carry

    lax.fori_loop(1, 256, greet, 0, unroll=5)

    live = lax.broadcasted_iota(jnp.int32, (8, 8, 32), 1) < count_ref[...][:, None, :]
    index = jnp.where(live, slots_ref[...], -1).reshape(64, 32)
    for i in range(32):
        col[i] = jnp.broadcast_to(index[:, i : i + 1], (64, 128)).astype(jnp.int16)
    turned = jnp.transpose(index)
    for n in range(16):
        lanes[n : n + 1, :] = jnp.concatenate([turned[2 * n : 2 * n + 1], turned[2 * n + 1 : 2 * n + 2]], axis=1)
    load_feat.wait()

    def pick(dz):
        n = (z + dz) % 8
        slab = col[pl.ds(4 * n, 4)].reshape(256, 128)
        lane = lax.broadcasted_iota(jnp.int32, (256, 128), 1)
        acc = jnp.zeros((256, 256), F32)
        for c in range(8):
            halves = [slab == (lane + 256 * c + 128 * u).astype(jnp.int16) for u in range(2)]
            hot = jnp.concatenate([jnp.where(half, BF16(1), BF16(0)) for half in halves], axis=1)
            acc = acc + dot(hot, feat[2 * c : 2 * c + 2].reshape(256, 256))
        outb[pl.ds(n * 32, 32)] = to_blocks(acc)

    pick(ROUNDS[0][0])
    pl.semaphore_wait(barrier, 255)

    def send_round(steps, src, dst, ssem, rsem):
        def send(m, carry):
            h = ((cx + m // 8) % 4) * 2 + (cc + m // 4) % 2
            for dz in steps:
                i = ((z + dz) % 8) * 4 + (y + m) % 4
                pltpu.make_async_remote_copy(
                    src.at[i * 8 + h], dst.at[me], ssem.at[dz], rsem.at[dz], device_id=h * 32 + i, device_id_type=FLAT
                ).start()
            return carry

        if steps[0] == 0:
            lax.fori_loop(1, 32, send, 0)
        else:
            lax.fori_loop(0, 32, send, 0, unroll=2)

    def plane(dz, src, dst, ssem, rsem):
        n = 32 if dz else 31
        return pltpu.make_async_remote_copy(
            src.at[pl.ds(0, n)], dst.at[pl.ds(0, n)], ssem.at[dz], rsem.at[dz], device_id=flat, device_id_type=FLAT
        )

    for steps in ROUNDS:
        for dz in steps:
            if dz != ROUNDS[0][0]:
                pick(dz)
        send_round(steps, outb, halob, s1, q1)
    own1 = pltpu.make_async_copy(outb.at[me], halob.at[me], lsem.at[3])
    own1.start()

    load_adj.wait()

    def prepare(b, carry):
        rows = pl.ds(pl.multiple_of(b * EDGE, EDGE), EDGE)
        a0 = adj[b, 0].astype(F32)
        a1 = adj[b, 1].astype(F32)
        degree = jnp.sum(a0 + a1, axis=1, keepdims=True)
        inv[rows, :] = jnp.broadcast_to(1.0 / jnp.maximum(degree, 1.0), (EDGE, EDGE))
        adj1[b] = a1.astype(BF16)
        t0 = ts_ref[0, b]
        t1 = jnp.maximum(ts_ref[1, b] - TILES, 0)
        block = feat[t0]
        s_own[rows, :] = dot(a0.astype(BF16), block)
        p_self[rows, :] = dot(feat[b], ws_ref[...]) + bias_ref[...]
        a0t = jnp.transpose(a0)
        a1t = jnp.transpose(a1)
        own = jnp.broadcast_to(t0, (EDGE, EDGE))
        far = jnp.broadcast_to(t1, (EDGE, EDGE))
        for e in range(TILES):
            at_own[e * EDGE : (e + 1) * EDGE, rows] = jnp.where(own == e, a0t, 0.0).astype(BF16)
            at_halo[e * EDGE : (e + 1) * EDGE, rows] = jnp.where(far == e, a1t, 0.0).astype(BF16)
        return carry

    lax.fori_loop(0, TILES, prepare, 0)

    def spread(n, carry):
        slots = jnp.concatenate([lanes[pl.ds(2 * n, 1), :], lanes[pl.ds(2 * n + 1, 1), :]], axis=1)
        line = lax.broadcasted_iota(jnp.int32, (256, 256), 0).astype(jnp.int16)
        for c in range(8):
            here = jnp.broadcast_to(slots - 256 * c, (256, 256)).astype(jnp.int16)
            hot = jnp.where(here == line, BF16(1), BF16(0))
            oht[256 * c : 256 * c + 256, pl.ds(pl.multiple_of(n * 256, 256), 256)] = hot
        return carry

    lax.fori_loop(0, 8, spread, 0)
    load_gout.wait()

    halo[...] = jnp.zeros_like(halo)

    def take(steps):
        for dz in steps:
            plane(dz, outb, halob, s1, q1).wait_recv()
            n = (z + 8 - dz) % 8
            halo[pl.ds(2 * n, 2)] = from_blocks(halob[pl.ds(n * 32, 32)]).reshape(2, EDGE, WIDTH)

    def layer(b, carry):
        rows = pl.ds(pl.multiple_of(b * 256, 256), 256)
        sums = []
        for u in range(2):
            t1 = jnp.maximum(ts_ref[1, 2 * b + u] - TILES, 0)
            block = halo[t1]
            sums.append(dot(adj1[2 * b + u], block))
        scale = inv[rows, :]
        scale = jnp.concatenate([scale, scale], axis=1)
        m = ((s_own[rows, :] + jnp.concatenate(sums, axis=0)) * scale).astype(BF16)
        mean[rows, :] = m
        pre = p_self[rows, :] + dot(m, wn_ref[...])
        sigma = 0.5 + 0.5 * jnp.tanh(0.5 * pre)
        out_ref[rows, :] = (pre * sigma).astype(BF16)
        slope = sigma * (1.0 + pre * (1.0 - sigma))
        gp = (gout[rows, :].astype(F32) * slope).astype(BF16)
        gpre[rows, :] = gp
        gagg[rows, :] = (dot_cols(gp, wn_ref[...]) * scale).astype(BF16)
        return carry

    def give_back(steps):
        for dz in steps:
            n = (z + dz) % 8
            rows = pl.ds(pl.multiple_of(n * 256, 256), 256)
            acc = jnp.zeros((256, 256), F32)
            for c in range(8):
                acc = acc + dot(at_halo[rows, 256 * c : 256 * c + 256], gagg[256 * c : 256 * c + 256, :])
            outg[pl.ds(n * 32, 32)] = to_blocks(acc)
        send_round(steps, outg, retb, s2, q2)

    for steps in ROUNDS[:EARLY]:
        take(steps)
    lax.fori_loop(0, 8, layer, 0, unroll=4)
    for steps in ROUNDS[:EARLY]:
        give_back(steps)
    own1.wait()
    for steps in ROUNDS[EARLY:]:
        take(steps)
    lax.fori_loop(0, 8, layer, 0, unroll=4)

    def weights(c, carry):
        acc_self, acc_neigh, acc_bias = carry
        rows = pl.ds(pl.multiple_of(c * 256, 256), 256)
        gp = gpre[rows, :]
        acc_self = acc_self + dot_rows(feat[pl.ds(2 * c, 2)].reshape(256, 256), gp)
        acc_neigh = acc_neigh + dot_rows(mean[rows, :], gp)
        acc_bias = acc_bias + jnp.sum(gp.astype(F32).reshape(32, 8, 256), axis=0)
        return acc_self, acc_neigh, acc_bias

    zero = jnp.zeros((256, 256), F32)
    acc_self, acc_neigh, acc_bias = lax.fori_loop(0, 8, weights, (zero, zero, jnp.zeros((8, 256), F32)))
    part[0:16] = acc_self.reshape(16, 16, WIDTH)
    part[16:32] = acc_neigh.reshape(16, 16, WIDTH)
    bias_row = jnp.sum(acc_bias, axis=0, keepdims=True)

    spot = g * 4 + y
    b_shares[spot] = jnp.concatenate([bias_row[:, :128], bias_row[:, 128:], jnp.zeros((6, 128), F32)], axis=0)

    def send_share(t, carry):
        o = lax.rem(spot + t, OWNERS)
        pltpu.make_async_remote_copy(
            part.at[o], shares.at[spot], sr.at[0], qr.at[0], device_id=(o // 4) * 32 + z * 4 + o % 4, device_id_type=FLAT
        ).start()
        return carry

    lax.fori_loop(1, OWNERS, send_share, 0)
    shares[spot] = part[spot]

    @pl.when(spot != 0)
    def _():
        pltpu.make_async_remote_copy(
            b_shares.at[spot], b_shares.at[spot], sr.at[3], qr.at[3], device_id=z * 4, device_id_type=FLAT
        ).start()

    for steps in ROUNDS[EARLY:]:
        give_back(steps)
    own2 = pltpu.make_async_copy(outg.at[me], retb.at[me], lsem.at[5])
    own2.start()

    def batch(n, sem, dst):
        return pltpu.make_async_remote_copy(
            dst.at[pl.ds(0, n)], dst.at[pl.ds(0, n)], sr.at[sem], qr.at[sem], device_id=flat, device_id_type=FLAT
        )

    batch(31, 0, shares).wait_recv()
    acc = shares[0]
    for o in range(1, OWNERS):
        acc = acc + shares[o]
    layers[z] = acc

    def send_layer(t, carry):
        to = lax.rem(z + t, 8)
        pltpu.make_async_remote_copy(
            layers.at[z], layers.at[z], sr.at[1], qr.at[1], device_id=g * 32 + to * 4 + y, device_id_type=FLAT
        ).start()
        return carry

    lax.fori_loop(1, 8, send_layer, 0)

    @pl.when(spot == 0)
    def _():
        batch(31, 3, b_shares).wait_recv()
        total_bias = b_shares[0]
        for o in range(1, OWNERS):
            total_bias = total_bias + b_shares[o]
        b_layers[z] = total_bias

        def send_bias(t, carry):
            to = lax.rem(z + t, 8)
            pltpu.make_async_remote_copy(
                b_layers.at[z], b_layers.at[z], sr.at[4], qr.at[4], device_id=to * 4, device_id_type=FLAT
            ).start()
            return carry

        lax.fori_loop(1, 8, send_bias, 0)

    def settle(steps, last=False):
        planes, spots = [], []
        for dz in steps:
            plane(dz, outg, retb, s2, q2).wait_recv()
            n = (z + 8 - dz) % 8
            planes.append(from_blocks(retb[pl.ds(n * 32, 32)]))
            spots.append(pl.ds(pl.multiple_of(n * 256, 256), 256))
        for c in range(8):
            at = slice(256 * c, 256 * c + 256)
            acc = total[at, :]
            for place, rows in zip(spots, planes):
                acc = acc + dot(oht[at, place], rows)
            if last:
                gf_ref[at, :] = acc.astype(BF16)
            else:
                total[at, :] = acc

    def base(n, carry):
        rows = pl.ds(pl.multiple_of(n * 256, 256), 256)
        acc = dot_cols(gpre[rows, :], ws_ref[...])
        for c in range(8):
            acc = acc + dot(at_own[rows, 256 * c : 256 * c + 256], gagg[256 * c : 256 * c + 256, :])
        total[rows, :] = acc
        return carry

    lax.fori_loop(0, 8, base, 0)

    batch(7, 1, layers).wait_recv()
    acc = layers[0]
    for k in range(1, 8):
        acc = acc + layers[k]
    factor = 1.0 / math.sqrt(ROWS * 256)
    done[spot] = (acc * factor).astype(done.dtype)

    def send_done(t, carry):
        o = lax.rem(spot + t, OWNERS)
        pltpu.make_async_remote_copy(
            done.at[spot], done.at[spot], sr.at[2], qr.at[2], device_id=(o // 4) * 32 + z * 4 + o % 4, device_id_type=FLAT
        ).start()
        return carry

    lax.fori_loop(1, OWNERS, send_done, 0)

    @pl.when(spot == 0)
    def _():
        batch(7, 4, b_layers).wait_recv()
        total_bias = b_layers[0]
        for k in range(1, 8):
            total_bias = total_bias + b_layers[k]
        b_done[0] = total_bias * factor

        def send_bias(o, carry):
            pltpu.make_async_remote_copy(
                b_done.at[0], b_done.at[0], sr.at[5], qr.at[5], device_id=(o // 4) * 32 + z * 4 + o % 4, device_id_type=FLAT
            ).start()
            return carry

        lax.fori_loop(1, OWNERS, send_bias, 0)

    settle(ROUNDS[0])
    settle(ROUNDS[1])
    settle(ROUNDS[2])
    settle(ROUNDS[3])
    own2.wait()
    settle(ROUNDS[4], True)

    batch(31, 2, done).wait_recv()
    gs_ref[...] = done[0:16].astype(F32).reshape(WIDTH, WIDTH)
    gn_ref[...] = done[16:32].astype(F32).reshape(WIDTH, WIDTH)

    @pl.when(spot != 0)
    def _():
        batch(1, 5, b_done).wait_recv()

    gb_ref[:, :128] = b_done[0, 0:1]
    gb_ref[:, 128:] = b_done[0, 1:2]

    for dz in range(8):
        plane(dz, outb, halob, s1, q1).wait_send()
        plane(dz, outg, retb, s2, q2).wait_send()
    batch(31, 0, shares).wait_send()
    batch(7, 1, layers).wait_send()
    batch(31, 2, done).wait_send()

    @pl.when(spot != 0)
    def _():
        batch(1, 3, b_shares).wait_send()

    @pl.when(spot == 0)
    def _():
        batch(7, 4, b_layers).wait_send()
        batch(31, 5, b_shares).wait_send()


def hand_over(*refs):
    sems = refs[10]
    copies = [pltpu.make_async_copy(refs[n], refs[5 + n], sems.at[n]) for n in range(5)]
    for copy in copies:
        copy.start()
    for copy in copies:
        copy.wait()


def local(
    features, w_self, w_neigh, node_bias, grad_out, send_rows, send_count, adjacency, tile_source
):
    vmem, hbm = pl.BlockSpec(memory_space=pltpu.VMEM), pl.BlockSpec(memory_space=pl.ANY)
    tall = (ROWS, WIDTH)
    blocks = (256, 16, 128)
    dma = pltpu.SemaphoreType.DMA
    shapes = [
        jax.ShapeDtypeStruct(tall, BF16),
        jax.ShapeDtypeStruct(tall, BF16),
        jax.ShapeDtypeStruct((WIDTH, WIDTH), F32),
        jax.ShapeDtypeStruct((WIDTH, WIDTH), F32),
        jax.ShapeDtypeStruct((1, WIDTH), F32),
    ]
    made = pl.pallas_call(
        kernel,
        out_shape=[pltpu.VMEM(a.shape, a.dtype) for a in shapes],
        in_specs=[vmem, vmem, pl.BlockSpec(memory_space=pltpu.SMEM), vmem, vmem, vmem, hbm, hbm, hbm],
        out_specs=[vmem] * 5,
        scratch_shapes=[
            pltpu.VMEM((TILES, EDGE, WIDTH), BF16),
            pltpu.VMEM(tall, BF16),
            pltpu.VMEM((TILES, 2, EDGE, EDGE), jnp.int32),
            pltpu.VMEM((32, 64, 128), jnp.int16),
            pltpu.VMEM(blocks, BF16),
            pltpu.VMEM(blocks, BF16),
            pltpu.VMEM(blocks, BF16),
            pltpu.VMEM(blocks, BF16),
            pltpu.VMEM((TILES, EDGE, WIDTH), BF16),
            pltpu.VMEM((TILES, EDGE, EDGE), BF16),
            pltpu.VMEM((ROWS, ROWS), BF16),
            pltpu.VMEM((ROWS, ROWS), BF16),
            pltpu.VMEM((ROWS, EDGE), F32),
            pltpu.VMEM(tall, F32),
            pltpu.VMEM(tall, F32),
            pltpu.VMEM(tall, BF16),
            pltpu.VMEM(tall, BF16),
            pltpu.VMEM(tall, BF16),
            pltpu.VMEM(tall, F32),
            pltpu.VMEM((ROWS, ROWS), BF16),
            pltpu.VMEM((16, 128), jnp.int32),
            pltpu.VMEM((OWNERS, 16, WIDTH), F32),
            pltpu.VMEM((OWNERS, 16, WIDTH), F32),
            pltpu.VMEM((8, 16, WIDTH), F32),
            pltpu.VMEM((OWNERS, 16, WIDTH), BF16),
            pltpu.VMEM((OWNERS, 8, 128), F32),
            pltpu.VMEM((8, 8, 128), F32),
            pltpu.VMEM((1, 8, 128), F32),
            dma((7,)),
            dma((8,)),
            dma((8,)),
            dma((8,)),
            dma((8,)),
            dma((6,)),
            dma((6,)),
        ],
        compiler_params=pltpu.CompilerParams(
            collective_id=0, has_side_effects=True, vmem_limit_bytes=54 << 20
        ),
        name="sage_layer",
    )(
        send_rows[0].transpose(1, 2, 0), send_count[0].T, tile_source[0].T, node_bias.reshape(1, WIDTH), w_self, w_neigh, features.reshape(TILES, EDGE, WIDTH), grad_out, adjacency[0]
    )
    out, gf, gs, gn, gb = pl.pallas_call(
        hand_over,
        out_shape=shapes,
        in_specs=[vmem] * 5,
        out_specs=[hbm] * 5,
        scratch_shapes=[dma((5,))],
        compiler_params=pltpu.CompilerParams(vmem_limit_bytes=4 << 20),
        name="hand_over",
    )(*made)
    return out, gf, gs, gn, gb.reshape(WIDTH)


def solution(mesh):
    rows = P(("group", "inner"), None)
    placed = (
        rows,
        P(),
        P(),
        P(),
        rows,
        P(("group", "inner"), None, None, None),
        P(("group", "inner"), None, None),
        P(("group", "inner"), None, None, None, None),
        P(("group", "inner"), None, None),
    )
    return jax.shard_map(
        local, mesh=mesh, in_specs=placed, out_specs=(rows, rows, P(), P(), P()), check_vma=False
    )
```

```python
import math

import jax
import jax.numpy as jnp
from jax import lax
from jax.experimental import pallas as pl
from jax.experimental.pallas import tpu as pltpu
from jax.sharding import PartitionSpec as P

FLAT = pl.DeviceIdType.LOGICAL
BF16, F32 = jnp.bfloat16, jnp.float32
ROWS, WIDTH, EDGE, TILES = 2048, 256, 128, 16
OWNERS = 32
EARLY = 3


def step(u):
    return 4 + ((u + 1) // 2) * (1 - 2 * (u % 2))


def dot(left, right):
    return jnp.dot(left, right, preferred_element_type=F32)


def dot_rows(left, right):
    return lax.dot_general(left, right, (((0,), (0,)), ((), ())), preferred_element_type=F32)


def dot_cols(left, right):
    return lax.dot_general(left, right, (((1,), (1,)), ((), ())), preferred_element_type=F32)


def to_blocks(rows):
    left = rows[:, :128].reshape(32, 8, 128)
    right = rows[:, 128:].reshape(32, 8, 128)
    return jnp.concatenate([left, right], axis=1).astype(BF16)


def from_blocks(blocks):
    wide = blocks.astype(F32)
    rows = jnp.concatenate([wide[:, :8], wide[:, 8:]], axis=2)
    return rows.reshape(256, 256).astype(BF16)


def kernel(
    slots_ref, count_ref, ts_ref, bias_ref, ws_ref, wn_ref, feat_hbm, gout_hbm, adj_hbm,
    out_ref, gf_ref, gs_ref, gn_ref, gb_ref,
    feat, gout, adj, col, outb, halob, outg, retb, halo, adj1, at_own, at_halo, inv,
    s_own, p_self, mean, gpre, gagg, total,
    oht, lanes, part, shares, layers, done, b_shares, b_layers, b_done,
    lsem, s1, q1, s2, q2, sr, qr,
):
    g, j = lax.axis_index("group"), lax.axis_index("inner")
    z, y, cx, cc = j // 4, j % 4, g // 2, g % 2
    me, flat = j * 8 + g, g * 32 + j

    load_feat = pltpu.make_async_copy(feat_hbm, feat, lsem.at[0])
    load_adj = pltpu.make_async_copy(adj_hbm, adj, lsem.at[1])
    load_gout = pltpu.make_async_copy(gout_hbm, gout, lsem.at[2])
    load_feat.start()
    load_adj.start()
    load_gout.start()

    barrier = pltpu.get_barrier_semaphore()

    def greet(t, carry):
        d = lax.rem(flat + t, 256)
        pl.semaphore_signal(barrier, inc=1, device_id=d, device_id_type=FLAT)
        return carry

    lax.fori_loop(1, 256, greet, 0, unroll=5)

    live = lax.broadcasted_iota(jnp.int32, (8, 8, 32), 1) < count_ref[...][:, None, :]
    index = jnp.where(live, slots_ref[...], -1).reshape(64, 32)
    for i in range(32):
        col[i] = jnp.broadcast_to(index[:, i : i + 1], (64, 128)).astype(jnp.int16)
    turned = jnp.transpose(index)
    for n in range(16):
        lanes[n : n + 1, :] = jnp.concatenate([turned[2 * n : 2 * n + 1], turned[2 * n + 1 : 2 * n + 2]], axis=1)
    load_feat.wait()

    def pick(u):
        n = (z + step(u)) % 8
        slab = col[pl.ds(4 * n, 4)].reshape(256, 128)
        lane = lax.broadcasted_iota(jnp.int32, (256, 128), 1)
        acc = jnp.zeros((256, 256), F32)
        for c in range(8):
            halves = [slab == (lane + 256 * c + 128 * u).astype(jnp.int16) for u in range(2)]
            hot = jnp.concatenate([jnp.where(half, BF16(1), BF16(0)) for half in halves], axis=1)
            acc = acc + dot(hot, feat[2 * c : 2 * c + 2].reshape(256, 256))
        outb[pl.ds(n * 32, 32)] = to_blocks(acc)

    pick(0)
    pl.semaphore_wait(barrier, 255)

    def send_plane(u, src, dst, ssem, rsem):
        def send(m, carry):
            h = ((cx + m // 8) % 4) * 2 + (cc + m // 4) % 2
            i = ((z + step(u)) % 8) * 4 + (y + m) % 4
            pltpu.make_async_remote_copy(
                src.at[i * 8 + h], dst.at[me], ssem.at[u], rsem.at[u], device_id=h * 32 + i, device_id_type=FLAT
            ).start()
            return carry

        lax.fori_loop(u // 7, 32, send, 0)

    def plane(u, src, dst, ssem, rsem, n=32):
        return pltpu.make_async_remote_copy(
            src.at[pl.ds(0, n)], dst.at[pl.ds(0, n)], ssem.at[u], rsem.at[u], device_id=flat, device_id_type=FLAT
        )

    send_plane(0, outb, halob, s1, q1)

    def send_rows(u, carry):
        pick(u)
        send_plane(u, outb, halob, s1, q1)
        return carry

    lax.fori_loop(1, 8, send_rows, 0)
    own1 = pltpu.make_async_copy(outb.at[me], halob.at[me], lsem.at[3])
    own1.start()

    load_adj.wait()

    def prepare(b, carry):
        rows = pl.ds(pl.multiple_of(b * EDGE, EDGE), EDGE)
        a0 = adj[b, 0].astype(F32)
        a1 = adj[b, 1].astype(F32)
        degree = jnp.sum(a0 + a1, axis=1, keepdims=True)
        inv[rows, :] = jnp.broadcast_to(1.0 / jnp.maximum(degree, 1.0), (EDGE, EDGE))
        adj1[b] = a1.astype(BF16)
        t0 = ts_ref[0, b]
        t1 = jnp.maximum(ts_ref[1, b] - TILES, 0)
        block = feat[t0]
        s_own[rows, :] = dot(a0.astype(BF16), block)
        p_self[rows, :] = dot(feat[b], ws_ref[...]) + bias_ref[...]
        a0t = jnp.transpose(a0)
        a1t = jnp.transpose(a1)
        own = jnp.broadcast_to(t0, (EDGE, EDGE))
        far = jnp.broadcast_to(t1, (EDGE, EDGE))
        for e in range(TILES):
            at_own[e * EDGE : (e + 1) * EDGE, rows] = jnp.where(own == e, a0t, 0.0).astype(BF16)
            at_halo[e * EDGE : (e + 1) * EDGE, rows] = jnp.where(far == e, a1t, 0.0).astype(BF16)
        return carry

    lax.fori_loop(0, TILES, prepare, 0)

    def spread(n, carry):
        slots = jnp.concatenate([lanes[pl.ds(2 * n, 1), :], lanes[pl.ds(2 * n + 1, 1), :]], axis=1)
        line = lax.broadcasted_iota(jnp.int32, (256, 256), 0).astype(jnp.int16)
        for c in range(8):
            here = jnp.broadcast_to(slots - 256 * c, (256, 256)).astype(jnp.int16)
            hot = jnp.where(here == line, BF16(1), BF16(0))
            oht[256 * c : 256 * c + 256, pl.ds(pl.multiple_of(n * 256, 256), 256)] = hot
        return carry

    lax.fori_loop(0, 8, spread, 0)
    load_gout.wait()

    halo[...] = jnp.zeros_like(halo)

    def place(u):
        n = (z + 8 - step(u)) % 8
        halo[pl.ds(2 * n, 2)] = from_blocks(halob[pl.ds(n * 32, 32)]).reshape(2, EDGE, WIDTH)

    def take(u, carry):
        plane(u, outb, halob, s1, q1).wait_recv()
        place(u)
        return carry

    def layer(b, carry):
        rows = pl.ds(pl.multiple_of(b * 256, 256), 256)
        sums = []
        for u in range(2):
            t1 = jnp.maximum(ts_ref[1, 2 * b + u] - TILES, 0)
            block = halo[t1]
            sums.append(dot(adj1[2 * b + u], block))
        scale = inv[rows, :]
        scale = jnp.concatenate([scale, scale], axis=1)
        m = ((s_own[rows, :] + jnp.concatenate(sums, axis=0)) * scale).astype(BF16)
        mean[rows, :] = m
        pre = p_self[rows, :] + dot(m, wn_ref[...])
        sigma = 0.5 + 0.5 * jnp.tanh(0.5 * pre)
        out_ref[rows, :] = (pre * sigma).astype(BF16)
        slope = sigma * (1.0 + pre * (1.0 - sigma))
        gp = (gout[rows, :].astype(F32) * slope).astype(BF16)
        gpre[rows, :] = gp
        gagg[rows, :] = (dot_cols(gp, wn_ref[...]) * scale).astype(BF16)
        return carry

    def give_back(u, carry):
        n = (z + step(u)) % 8
        rows = pl.ds(pl.multiple_of(n * 256, 256), 256)
        acc = jnp.zeros((256, 256), F32)
        for c in range(8):
            acc = acc + dot(at_halo[rows, 256 * c : 256 * c + 256], gagg[256 * c : 256 * c + 256, :])
        outg[pl.ds(n * 32, 32)] = to_blocks(acc)
        send_plane(u, outg, retb, s2, q2)
        return carry

    lax.fori_loop(0, EARLY, take, 0)
    lax.fori_loop(0, 8, layer, 0, unroll=2)
    lax.fori_loop(0, EARLY, give_back, 0)
    lax.fori_loop(EARLY, 7, take, 0)
    own1.wait()
    plane(7, outb, halob, s1, q1, 31).wait_recv()
    place(7)
    lax.fori_loop(0, 8, layer, 0, unroll=2)

    def weights(c, carry):
        acc_self, acc_neigh, acc_bias = carry
        rows = pl.ds(pl.multiple_of(c * 256, 256), 256)
        gp = gpre[rows, :]
        acc_self = acc_self + dot_rows(feat[pl.ds(2 * c, 2)].reshape(256, 256), gp)
        acc_neigh = acc_neigh + dot_rows(mean[rows, :], gp)
        acc_bias = acc_bias + jnp.sum(gp.astype(F32).reshape(32, 8, 256), axis=0)
        return acc_self, acc_neigh, acc_bias

    zero = jnp.zeros((256, 256), F32)
    acc_self, acc_neigh, acc_bias = lax.fori_loop(0, 8, weights, (zero, zero, jnp.zeros((8, 256), F32)))
    part[0:16] = acc_self.reshape(16, 16, WIDTH)
    part[16:32] = acc_neigh.reshape(16, 16, WIDTH)
    bias_row = jnp.sum(acc_bias, axis=0, keepdims=True)

    spot = g * 4 + y
    b_shares[spot] = jnp.concatenate([bias_row[:, :128], bias_row[:, 128:], jnp.zeros((6, 128), F32)], axis=0)

    def send_share(t, carry):
        o = lax.rem(spot + t, OWNERS)
        pltpu.make_async_remote_copy(
            part.at[o], shares.at[spot], sr.at[0], qr.at[0], device_id=(o // 4) * 32 + z * 4 + o % 4, device_id_type=FLAT
        ).start()
        return carry

    lax.fori_loop(1, OWNERS, send_share, 0)
    shares[spot] = part[spot]

    @pl.when(spot != 0)
    def _():
        pltpu.make_async_remote_copy(
            b_shares.at[spot], b_shares.at[spot], sr.at[3], qr.at[3], device_id=z * 4, device_id_type=FLAT
        ).start()

    lax.fori_loop(EARLY, 8, give_back, 0)
    own2 = pltpu.make_async_copy(outg.at[me], retb.at[me], lsem.at[5])
    own2.start()

    def batch(n, sem, dst):
        return pltpu.make_async_remote_copy(
            dst.at[pl.ds(0, n)], dst.at[pl.ds(0, n)], sr.at[sem], qr.at[sem], device_id=flat, device_id_type=FLAT
        )

    batch(31, 0, shares).wait_recv()
    acc = shares[0]
    for o in range(1, OWNERS):
        acc = acc + shares[o]
    layers[z] = acc

    def send_layer(t, carry):
        to = lax.rem(z + t, 8)
        pltpu.make_async_remote_copy(
            layers.at[z], layers.at[z], sr.at[1], qr.at[1], device_id=g * 32 + to * 4 + y, device_id_type=FLAT
        ).start()
        return carry

    lax.fori_loop(1, 8, send_layer, 0)

    @pl.when(spot == 0)
    def _():
        batch(31, 3, b_shares).wait_recv()
        total_bias = b_shares[0]
        for o in range(1, OWNERS):
            total_bias = total_bias + b_shares[o]
        b_layers[z] = total_bias

        def send_bias(t, carry):
            to = lax.rem(z + t, 8)
            pltpu.make_async_remote_copy(
                b_layers.at[z], b_layers.at[z], sr.at[4], qr.at[4], device_id=to * 4, device_id_type=FLAT
            ).start()
            return carry

        lax.fori_loop(1, 8, send_bias, 0)

    def settle(u, last=False):
        plane(u, outg, retb, s2, q2, 31 if last else 32).wait_recv()
        n = (z + 8 - step(u)) % 8
        rows = from_blocks(retb[pl.ds(n * 32, 32)])
        spots = pl.ds(pl.multiple_of(n * 256, 256), 256)
        for c in range(8):
            at = slice(256 * c, 256 * c + 256)
            acc = total[at, :] + dot(oht[at, spots], rows)
            if last:
                gf_ref[at, :] = acc.astype(BF16)
            else:
                total[at, :] = acc

    def settle_one(u, carry):
        settle(u)
        return carry

    def base(n, carry):
        rows = pl.ds(pl.multiple_of(n * 256, 256), 256)
        acc = dot_cols(gpre[rows, :], ws_ref[...])
        for c in range(8):
            acc = acc + dot(at_own[rows, 256 * c : 256 * c + 256], gagg[256 * c : 256 * c + 256, :])
        total[rows, :] = acc
        return carry

    lax.fori_loop(0, 8, base, 0)

    batch(7, 1, layers).wait_recv()
    acc = layers[0]
    for k in range(1, 8):
        acc = acc + layers[k]
    factor = 1.0 / math.sqrt(ROWS * 256)
    done[spot] = (acc * factor).astype(done.dtype)

    def send_done(t, carry):
        o = lax.rem(spot + t, OWNERS)
        pltpu.make_async_remote_copy(
            done.at[spot], done.at[spot], sr.at[2], qr.at[2], device_id=(o // 4) * 32 + z * 4 + o % 4, device_id_type=FLAT
        ).start()
        return carry

    lax.fori_loop(1, OWNERS, send_done, 0)

    @pl.when(spot == 0)
    def _():
        batch(7, 4, b_layers).wait_recv()
        total_bias = b_layers[0]
        for k in range(1, 8):
            total_bias = total_bias + b_layers[k]
        b_done[0] = total_bias * factor

        def send_bias(o, carry):
            pltpu.make_async_remote_copy(
                b_done.at[0], b_done.at[0], sr.at[5], qr.at[5], device_id=(o // 4) * 32 + z * 4 + o % 4, device_id_type=FLAT
            ).start()
            return carry

        lax.fori_loop(1, OWNERS, send_bias, 0)

    lax.fori_loop(0, 7, settle_one, 0)
    own2.wait()
    settle(7, True)

    batch(31, 2, done).wait_recv()
    gs_ref[...] = done[0:16].astype(F32).reshape(WIDTH, WIDTH)
    gn_ref[...] = done[16:32].astype(F32).reshape(WIDTH, WIDTH)

    @pl.when(spot != 0)
    def _():
        batch(1, 5, b_done).wait_recv()

    gb_ref[:, :128] = b_done[0, 0:1]
    gb_ref[:, 128:] = b_done[0, 1:2]

    for u in range(8):
        plane(u, outb, halob, s1, q1, 31 if u == 7 else 32).wait_send()
        plane(u, outg, retb, s2, q2, 31 if u == 7 else 32).wait_send()
    batch(31, 0, shares).wait_send()
    batch(7, 1, layers).wait_send()
    batch(31, 2, done).wait_send()

    @pl.when(spot != 0)
    def _():
        batch(1, 3, b_shares).wait_send()

    @pl.when(spot == 0)
    def _():
        batch(7, 4, b_layers).wait_send()
        batch(31, 5, b_shares).wait_send()


def hand_over(*refs):
    sems = refs[10]
    copies = [pltpu.make_async_copy(refs[n], refs[5 + n], sems.at[n]) for n in range(5)]
    for copy in copies:
        copy.start()
    for copy in copies:
        copy.wait()


def local(
    features, w_self, w_neigh, node_bias, grad_out, send_rows, send_count, adjacency, tile_source
):
    vmem, hbm = pl.BlockSpec(memory_space=pltpu.VMEM), pl.BlockSpec(memory_space=pl.ANY)
    tall = (ROWS, WIDTH)
    blocks = (256, 16, 128)
    dma = pltpu.SemaphoreType.DMA
    shapes = [
        jax.ShapeDtypeStruct(tall, BF16),
        jax.ShapeDtypeStruct(tall, BF16),
        jax.ShapeDtypeStruct((WIDTH, WIDTH), F32),
        jax.ShapeDtypeStruct((WIDTH, WIDTH), F32),
        jax.ShapeDtypeStruct((1, WIDTH), F32),
    ]
    made = pl.pallas_call(
        kernel,
        out_shape=[pltpu.VMEM(a.shape, a.dtype) for a in shapes],
        in_specs=[vmem, vmem, pl.BlockSpec(memory_space=pltpu.SMEM), vmem, vmem, vmem, hbm, hbm, hbm],
        out_specs=[vmem] * 5,
        scratch_shapes=[
            pltpu.VMEM((TILES, EDGE, WIDTH), BF16),
            pltpu.VMEM(tall, BF16),
            pltpu.VMEM((TILES, 2, EDGE, EDGE), jnp.int32),
            pltpu.VMEM((32, 64, 128), jnp.int16),
            pltpu.VMEM(blocks, BF16),
            pltpu.VMEM(blocks, BF16),
            pltpu.VMEM(blocks, BF16),
            pltpu.VMEM(blocks, BF16),
            pltpu.VMEM((TILES, EDGE, WIDTH), BF16),
            pltpu.VMEM((TILES, EDGE, EDGE), BF16),
            pltpu.VMEM((ROWS, ROWS), BF16),
            pltpu.VMEM((ROWS, ROWS), BF16),
            pltpu.VMEM((ROWS, EDGE), F32),
            pltpu.VMEM(tall, F32),
            pltpu.VMEM(tall, F32),
            pltpu.VMEM(tall, BF16),
            pltpu.VMEM(tall, BF16),
            pltpu.VMEM(tall, BF16),
            pltpu.VMEM(tall, F32),
            pltpu.VMEM((ROWS, ROWS), BF16),
            pltpu.VMEM((16, 128), jnp.int32),
            pltpu.VMEM((OWNERS, 16, WIDTH), F32),
            pltpu.VMEM((OWNERS, 16, WIDTH), F32),
            pltpu.VMEM((8, 16, WIDTH), F32),
            pltpu.VMEM((OWNERS, 16, WIDTH), BF16),
            pltpu.VMEM((OWNERS, 8, 128), F32),
            pltpu.VMEM((8, 8, 128), F32),
            pltpu.VMEM((1, 8, 128), F32),
            dma((7,)),
            dma((8,)),
            dma((8,)),
            dma((8,)),
            dma((8,)),
            dma((6,)),
            dma((6,)),
        ],
        compiler_params=pltpu.CompilerParams(
            collective_id=0, has_side_effects=True, vmem_limit_bytes=54 << 20
        ),
        name="sage_layer",
    )(
        send_rows[0].transpose(1, 2, 0), send_count[0].T, tile_source[0].T, node_bias.reshape(1, WIDTH), w_self, w_neigh, features.reshape(TILES, EDGE, WIDTH), grad_out, adjacency[0]
    )
    out, gf, gs, gn, gb = pl.pallas_call(
        hand_over,
        out_shape=shapes,
        in_specs=[vmem] * 5,
        out_specs=[hbm] * 5,
        scratch_shapes=[dma((5,))],
        compiler_params=pltpu.CompilerParams(vmem_limit_bytes=4 << 20),
        name="hand_over",
    )(*made)
    return out, gf, gs, gn, gb.reshape(WIDTH)


def solution(mesh):
    rows = P(("group", "inner"), None)
    placed = (
        rows,
        P(),
        P(),
        P(),
        rows,
        P(("group", "inner"), None, None, None),
        P(("group", "inner"), None, None),
        P(("group", "inner"), None, None, None, None),
        P(("group", "inner"), None, None),
    )
    return jax.shard_map(
        local, mesh=mesh, in_specs=placed, out_specs=(rows, rows, P(), P(), P()), check_vma=False
    )
```
